512 devices in a mesh: dp: 32 (over z, x), expert: 16 (over y, core).
Axes of the slice: x: 4, y: 8, z: 8, core: 2. Of those that a mesh axis runs over, the one named last changes fastest.
Arguments:
- tokens: bfloat16 [65536, 1024], P(('dp', 'expert')), may hold values from -6 to 6
- route_ids: int32 [65536, 8], P(('dp', 'expert')), may hold values from 0 to 127, as said below
- route_weights: float32 [65536, 8], P(('dp', 'expert')), may hold values from 0.05 to 1
- upstream: bfloat16 [65536, 1024], P(('dp', 'expert')), may hold values from -6 to 6
- w_gate: bfloat16 [16, 1024, 384], P('expert', 'dp'), may hold values from -0.1875 to 0.1875
- w_up: bfloat16 [16, 1024, 384], P('expert', 'dp'), may hold values from -0.1875 to 0.1875
- w_down: bfloat16 [16, 384, 1024], P('expert', 'dp'), may hold values from -0.3125 to 0.3125
Outputs:
- mixed: bfloat16 [65536, 1024], P(('dp', 'expert'))
- grad_tokens: bfloat16 [65536, 1024], P(('dp', 'expert'))
- grad_route: float32 [65536, 8], P(('dp', 'expert'))
- grad_gate: bfloat16 [16, 1024, 384], P('expert', 'dp')
- grad_up: bfloat16 [16, 1024, 384], P('expert', 'dp')
- grad_down: bfloat16 [16, 384, 1024], P('expert', 'dp')
The draws below stay inside these ranges and needn't reach their ends.
Inputs may be any that keep to these rules, and one draw needn't show every extreme that they name: `route_ids`: the k-th id of every row lies in [k * 16, (k + 1) * 16). Among the rows of one device no id is named by more than 16 rows, and in each band of ids some id is named by exactly 16 of them.
All inputs are finite; a program needn't handle non-finite values.
Results may differ from the reference program's by a relative error of at most 0.023.
Values may be sent and summed in bfloat16 or wider, within the bound.
No kernel may reach another device: no remote copies, remote signals or barrier semaphores. Data moves between devices by JAX's collectives and lax.ppermute only.
A program may use at most 64 MiB of HBM per device.

```python
import math
import jax
import jax.numpy as jnp
from jax import lax

D = 1024
FF = 384
EXPERTS = 128
TOP = 8
TOK_DEV = 128
SLOT_CAP = 16
FLIGHT = 16
TOKENS = 65536
N_DP = 32
N_EXPERT = 16


def draw_route_ids(key, part):
    key = jax.random.fold_in(key, 11)
    band = EXPERTS // TOP
    pairs = band // 2
    mean_rows = TOK_DEV // band
    blocks = TOKENS // TOK_DEV
    key_sizes, key_ids, key_rows = jax.random.split(key, 3)
    spread = jax.random.randint(key_sizes, (blocks, TOP, pairs), 0, mean_rows)
    spread = spread.at[:, :, 0].set(mean_rows)
    counts = jnp.concatenate([mean_rows + spread, mean_rows - spread], axis=2)
    bounds = jnp.cumsum(counts, axis=2)
    positions = jnp.arange(TOK_DEV, dtype=jnp.int32)
    klass = jnp.sum((positions[None, None, :, None] >= bounds[:, :, None, :]).astype(jnp.int32), axis=3)
    id_scores = jax.random.randint(key_ids, (blocks, TOP, band), 0, 1 << 20) * band + jnp.arange(band, dtype=jnp.int32)
    id_order = jnp.argsort(id_scores, axis=2)
    row_scores = jax.random.randint(key_rows, (blocks, TOP, TOK_DEV), 0, 1 << 20) * TOK_DEV + positions
    row_place = jnp.argsort(jnp.argsort(row_scores, axis=2), axis=2)
    row_class = jnp.take_along_axis(klass, row_place, axis=2)
    local_ids = jnp.take_along_axis(id_order, row_class, axis=2)
    full_ids = local_ids + band * jnp.arange(TOP, dtype=jnp.int32)[None, :, None]
    return jnp.transpose(full_ids, (0, 2, 1)).reshape(blocks * TOK_DEV, TOP).astype(jnp.int32)


def shard_levels(own_key, extent, cuts, smallest, largest):
    level = 1.0
    for dim, blocks in cuts:
        heights = jax.random.uniform(jax.random.fold_in(jax.random.fold_in(own_key, 6), dim), (blocks,), jnp.float32, smallest / len(cuts), largest / len(cuts))
        level = level * jnp.repeat(jnp.exp(heights), extent[dim] // blocks).reshape((-1,) + (1,) * (len(extent) - 1 - dim))
    return level


def scatter_about(key, dims, scale, reach, shards=(), held_as=jnp.bfloat16):
    loudness = shard_levels(key, dims, shards, -0.22, 0.18) if shards else 1.0
    entries = jax.random.normal(key, dims, jnp.float32) * scale * loudness
    return jnp.minimum(jnp.maximum(entries, -reach), reach).astype(held_as)


def setup_inputs(seed: int = 0) -> dict:
    key_list = jax.random.split(jax.random.key(seed), 8)
    tokens = scatter_about(key_list[0], (TOKENS, D), 1.0, 6.0, ((0, 512),))
    route_ids = draw_route_ids(jax.random.fold_in(key_list[7], 71), 0)
    route_weights = jnp.clip(jnp.exp(math.log(1.0) - 2.9957323 * jax.random.uniform(key_list[2], (TOKENS, TOP), jnp.float32) ** shard_levels(key_list[2], (TOKENS, TOP), ((0, 512),), -0.2, 0.2)), 0.05, 1.0)
    upstream = scatter_about(key_list[3], (TOKENS, D), 1.0, 6.0, ((0, 512),))
    w_gate = scatter_about(key_list[4], (FLIGHT, D, FF), D ** -0.5, 0.1875, ((0, 16), (1, 32)))
    w_up = scatter_about(key_list[5], (FLIGHT, D, FF), D ** -0.5, 0.1875, ((0, 16), (1, 32)))
    w_down = scatter_about(key_list[6], (FLIGHT, FF, D), FF ** -0.5, 0.3125, ((0, 16), (1, 32)))
    return dict(tokens=tokens, route_ids=route_ids, route_weights=route_weights, upstream=upstream, w_gate=w_gate, w_up=w_up, w_down=w_down)


def expert_forward(rows, gate_mat, up_mat, down_mat):
    pre_gate = jnp.dot(rows, gate_mat, preferred_element_type=jnp.float32)
    pre_up = jnp.dot(rows, up_mat, preferred_element_type=jnp.float32)
    hidden = (jax.nn.silu(pre_gate) * pre_up).astype(jnp.bfloat16)
    outputs = jnp.dot(hidden, down_mat, preferred_element_type=jnp.float32).astype(jnp.bfloat16)
    return outputs, pre_gate, pre_up, hidden


def expert_backward(rows, scaled, pre_gate, pre_up, hidden, gate_mat, up_mat, down_mat):
    grad_hidden = jnp.dot(scaled, down_mat.T, preferred_element_type=jnp.float32)
    sigma = jax.nn.sigmoid(pre_gate)
    grad_gate_pre = (grad_hidden * pre_up * sigma * (1.0 + pre_gate * (1.0 - sigma))).astype(jnp.bfloat16)
    grad_up_pre = (grad_hidden * jax.nn.silu(pre_gate)).astype(jnp.bfloat16)
    row_grads = (jnp.dot(grad_gate_pre, gate_mat.T, preferred_element_type=jnp.float32)
                 + jnp.dot(grad_up_pre, up_mat.T, preferred_element_type=jnp.float32)).astype(jnp.bfloat16)
    part_gate = jnp.dot(rows.T, grad_gate_pre, preferred_element_type=jnp.float32)
    part_up = jnp.dot(rows.T, grad_up_pre, preferred_element_type=jnp.float32)
    part_down = jnp.dot(hidden.T, scaled, preferred_element_type=jnp.float32)
    return row_grads, part_gate, part_up, part_down


def rounded_total(parts):
    narrow = lax.optimization_barrier(parts.astype(jnp.bfloat16))
    return jnp.sum(narrow.astype(jnp.float32), axis=0).astype(jnp.bfloat16)


def reference(tokens, route_ids, route_weights, upstream, w_gate, w_up, w_down):
    blocks = TOKENS // TOK_DEV
    rows_all = N_EXPERT * SLOT_CAP
    width = tokens.shape[1]
    experts_axis = jnp.arange(N_EXPERT, dtype=jnp.int32)
    live_route = route_ids < N_EXPERT
    named = jnp.any(route_ids[:, :, None] == experts_axis[None, None, :], axis=1).astype(jnp.int32)
    slot_rank = jnp.cumsum(named.reshape(blocks, TOK_DEV, N_EXPERT), axis=1).reshape(TOKENS, N_EXPERT) - 1
    clipped = jnp.clip(route_ids, 0, N_EXPERT - 1).astype(jnp.int32)
    slot = jnp.take_along_axis(slot_rank, clipped, axis=1).astype(jnp.int32)
    token_index = jnp.arange(TOKENS, dtype=jnp.int32)
    block_index = token_index // TOK_DEV
    data_index = (block_index // N_EXPERT).astype(jnp.int32)
    source_index = (block_index % N_EXPERT).astype(jnp.int32)
    buffer_row = jnp.clip(source_index[:, None] * SLOT_CAP + slot, 0, rows_all - 1).astype(jnp.int32)
    target = jnp.where(live_route, route_ids, N_EXPERT).astype(jnp.int32)
    expert_rows = jnp.zeros((N_EXPERT, N_DP, rows_all, width), jnp.bfloat16)
    scaled_grads = jnp.zeros((N_EXPERT, N_DP, rows_all, width), jnp.bfloat16)
    upstream_wide = upstream.astype(jnp.float32)
    for column in range(TOP):
        expert_rows = expert_rows.at[target[:, column], data_index, buffer_row[:, column]].set(tokens, mode="drop")
        scaled = (route_weights[:, column:column + 1] * upstream_wide).astype(jnp.bfloat16)
        scaled_grads = scaled_grads.at[target[:, column], data_index, buffer_row[:, column]].set(scaled, mode="drop")

    def per_expert(operands):
        rows_e, scaled_e, gate_mat, up_mat, down_mat = operands

        def per_shard(rows, scaled):
            outputs, pre_gate, pre_up, hidden = expert_forward(rows, gate_mat, up_mat, down_mat)
            row_grads, part_gate, part_up, part_down = expert_backward(
                rows, scaled, pre_gate, pre_up, hidden, gate_mat, up_mat, down_mat)
            return outputs, row_grads, part_gate, part_up, part_down

        outputs, row_grads, part_gate, part_up, part_down = jax.vmap(per_shard)(rows_e, scaled_e)
        return outputs, row_grads, rounded_total(part_gate), rounded_total(part_up), rounded_total(part_down)

    expert_out, row_grads, grad_gate, grad_up, grad_down = lax.map(
        per_expert, (expert_rows, scaled_grads, w_gate, w_up, w_down))
    flat_out = expert_out.reshape(N_EXPERT * N_DP * rows_all, width)
    flat_grads = row_grads.reshape(N_EXPERT * N_DP * rows_all, width)
    mixed = jnp.zeros((TOKENS, width), jnp.float32)
    grad_sum = jnp.zeros((TOKENS, width), jnp.float32)
    route_columns = []
    for column in range(TOP):
        alive = live_route[:, column]
        index = jnp.where(alive, (clipped[:, column] * N_DP + data_index) * rows_all + buffer_row[:, column], 0).astype(jnp.int32)
        picked = jnp.take(flat_out, index, axis=0).astype(jnp.float32)
        gate_weight = jnp.where(alive, route_weights[:, column], 0.0)
        mixed = mixed + gate_weight[:, None] * picked
        route_columns.append(jnp.where(alive, jnp.sum(upstream_wide * picked, axis=1), 0.0))
        grad_rows = jnp.take(flat_grads, index, axis=0).astype(jnp.float32)
        grad_sum = grad_sum + jnp.where(alive[:, None], grad_rows, 0.0)
    grad_route = jnp.stack(route_columns, axis=1).astype(jnp.float32)
    return (mixed.astype(jnp.bfloat16), grad_sum.astype(jnp.bfloat16), grad_route, grad_gate, grad_up, grad_down)
```

```python
import functools

import jax
import jax.numpy as jnp
from jax import lax
from jax.experimental import pallas as pl
from jax.experimental.pallas import tpu as pltpu
from jax.sharding import PartitionSpec as P

FLIGHT = 16
CAP = 16
NZ = 8
NX = 4
TOK = 128
D = 1024
FF = 384
ROWS = FLIGHT * CAP
FD = FF // (NZ * NX)
SH = D // (NZ * NX)
PW = 2 * FF + D // 2
BF = jnp.bfloat16
F32 = jnp.float32
MIB = 1 << 20


def dot(a, b, dims):
    return lax.dot_general(a, b, (dims, ((), ())), preferred_element_type=F32)


def nn(a, b):
    return dot(a, b, ((1,), (0,)))


def tn(a, b):
    return dot(a, b, ((0,), (0,)))


def nt(a, b):
    return dot(a, b, ((1,), (1,)))


def route_rows(ids_t, weights_t):
    live = ids_t < FLIGHT
    expert = jnp.sum(jnp.where(live, ids_t, 0), axis=0, keepdims=True)
    weight = jnp.sum(jnp.where(live, weights_t, 0.0), axis=0, keepdims=True)
    alive = jnp.max(live.astype(jnp.int32), axis=0, keepdims=True) > 0
    return live, expert, weight, alive


def place(ids_t, weights_t):
    live, expert, weight, alive = route_rows(ids_t, weights_t)
    named = (lax.broadcasted_iota(jnp.int32, (FLIGHT, TOK), 0) == expert) & alive
    before = lax.broadcasted_iota(jnp.int32, (TOK, TOK), 0) < lax.broadcasted_iota(
        jnp.int32, (TOK, TOK), 1
    )
    rank = nn(named.astype(F32).astype(BF), before.astype(F32).astype(BF))
    slot = jnp.sum(jnp.where(named, rank, 0.0), axis=0, keepdims=True).astype(jnp.int32)
    row = jnp.where(alive, expert * CAP + slot, -1)
    mask = lax.broadcasted_iota(jnp.int32, (ROWS, TOK), 0) == row
    return live, weight, mask


def column_of(row):
    eye = lax.broadcasted_iota(jnp.int32, (TOK, TOK), 0) == lax.broadcasted_iota(
        jnp.int32, (TOK, TOK), 1
    )
    return jnp.sum(jnp.where(eye, row, 0.0), axis=1, keepdims=True)


def row_of(column):
    eye = lax.broadcasted_iota(jnp.int32, (TOK, TOK), 0) == lax.broadcasted_iota(
        jnp.int32, (TOK, TOK), 1
    )
    return jnp.sum(jnp.where(eye, column, 0.0), axis=0, keepdims=True)


def pack_kernel(gate_ref, up_ref, down_ref, out_ref):
    out_ref[:, :FF] = gate_ref[...]
    out_ref[:, FF : 2 * FF] = up_ref[...]
    down = jnp.concatenate(
        [down_ref[...].astype(F32), jnp.zeros((16 - FD, D), F32)], axis=0
    ).astype(BF)
    out_ref[:16, 2 * FF :] = down[:, : D // 2]
    out_ref[16:, 2 * FF :] = down[:, D // 2 :]


def dispatch_kernel(ids_ref, weights_ref, tokens_ref, upstream_ref, out_ref):
    live, weight, mask = place(ids_ref[...], weights_ref[...])
    picker = mask.astype(F32).astype(BF)
    out_ref[:, :D] = nn(picker, tokens_ref[...]).astype(BF)
    row_weight = jnp.sum(jnp.where(mask, weight, 0.0), axis=1, keepdims=True)
    out_ref[:, D:] = (row_weight * nn(picker, upstream_ref[...])).astype(BF)


def expert_kernel(
    recv_ref,
    b0_ref,
    b1_ref,
    b2_ref,
    b3_ref,
    sent_ref,
    q0_ref,
    q1_ref,
    q2_ref,
    q3_ref,
    full,
    grads,
):
    place_dp = lax.axis_index("dp")
    z, x = place_dp // NX, place_dp % NX
    for k, block in enumerate((b0_ref, b1_ref, b2_ref, b3_ref)):
        x_from = lax.rem(x + (NX - k), NX)
        for d in range(NZ):
            z_from = lax.rem(z + (NZ - d), NZ)
            start = pl.multiple_of((z_from * NX + x_from) * SH, SH)
            full[pl.ds(start, SH), :] = block[d * SH : (d + 1) * SH, :]
    gate, up = full[:, :FF], full[:, FF : 2 * FF]
    column = lax.broadcasted_iota(jnp.int32, (FF, 16 * NZ * NX), 1)
    of_row = (column // 16) * FD + column % 16
    unpad = ((lax.broadcasted_iota(jnp.int32, (FF, 16 * NZ * NX), 0) == of_row) & (column % 16 < FD)).astype(F32).astype(BF)
    packed = full[:, 2 * FF :].reshape(NZ * NX, 2, 16, D // 2)
    left = nn(unpad, packed[:, 0].reshape(16 * NZ * NX, D // 2)).astype(BF)
    right = nn(unpad, packed[:, 1].reshape(16 * NZ * NX, D // 2)).astype(BF)
    down = jnp.concatenate([left, right], axis=1)
    rows, scaled = recv_ref[:, :D], recv_ref[:, D:]
    pre_gate = nn(rows, gate)
    pre_up = nn(rows, up)
    grad_hidden = nt(scaled, down)
    sigma = jax.nn.sigmoid(pre_gate)
    silu = pre_gate * sigma
    hidden = (silu * pre_up).astype(BF)
    sent_ref[:, :D] = nn(hidden, down).astype(BF)
    grad_gate_pre = (grad_hidden * pre_up * sigma * (1.0 + pre_gate * (1.0 - sigma))).astype(BF)
    grad_up_pre = (grad_hidden * silu).astype(BF)
    sent_ref[:, D:] = (nt(grad_gate_pre, gate) + nt(grad_up_pre, up)).astype(BF)
    grads[:, :FF] = tn(rows, grad_gate_pre).astype(BF)
    grads[:, FF : 2 * FF] = tn(rows, grad_up_pre).astype(BF)
    hidden_padded = nn(hidden, unpad).astype(BF)
    part_down = tn(hidden_padded, scaled).astype(BF)
    halves = jnp.stack(
        [
            part_down[:, : D // 2].reshape(NZ * NX, 16, D // 2),
            part_down[:, D // 2 :].reshape(NZ * NX, 16, D // 2),
        ],
        axis=1,
    )
    grads[:, 2 * FF :] = halves.reshape(D, D // 2)
    for k, quarter in enumerate((q0_ref, q1_ref, q2_ref, q3_ref)):
        x_to = lax.rem(x + k, NX)
        for i in range(NZ):
            start = pl.multiple_of((i * NX + x_to) * SH, SH)
            quarter[i * SH : (i + 1) * SH, :] = grads[pl.ds(start, SH), :]


def sum_x_kernel(a_ref, b_ref, c_ref, d_ref, *out_refs):
    z = lax.axis_index("dp") // NX
    for d, out in enumerate(out_refs):
        start = pl.multiple_of(lax.rem(z + d, NZ) * SH, SH)
        here = pl.ds(start, SH)
        total = a_ref[here, :].astype(F32) + b_ref[here, :].astype(F32)
        total = total + c_ref[here, :].astype(F32) + d_ref[here, :].astype(F32)
        out[...] = total.astype(BF)


def sum_z_kernel(*refs):
    parts, (gate_ref, up_ref, down_ref) = refs[:NZ], refs[NZ:]
    total = parts[0][...].astype(F32)
    for part in parts[1:]:
        total = total + part[...].astype(F32)
    gate_ref[...] = total[:, :FF].astype(BF)
    up_ref[...] = total[:, FF : 2 * FF].astype(BF)
    down_ref[:, : D // 2] = total[:FD, 2 * FF :].astype(BF)
    down_ref[:, D // 2 :] = total[16 : 16 + FD, 2 * FF :].astype(BF)


def combine_kernel(ids_ref, weights_ref, upstream_ref, home_ref, mixed_ref, tokens_ref, route_ref):
    live, weight, mask = place(ids_ref[...], weights_ref[...])
    picker = mask.astype(F32).astype(BF)
    tokens_ref[...] = tn(picker, home_ref[:, D:]).astype(BF)
    picked = tn(picker, home_ref[:, :D])
    mixed_ref[...] = (column_of(weight) * picked).astype(BF)
    inner = jnp.sum(upstream_ref[...].astype(F32) * picked, axis=1, keepdims=True)
    route_ref[...] = jnp.where(live, row_of(inner), 0.0)


def call(kernel, outs, scratch=(), vmem=None, flops=0, moved=1 * MIB):
    shapes = [jax.ShapeDtypeStruct(s, t) for s, t in outs]
    single = len(shapes) == 1
    return pl.pallas_call(
        kernel,
        out_shape=shapes[0] if single else shapes,
        scratch_shapes=list(scratch),
        compiler_params=pltpu.CompilerParams(vmem_limit_bytes=vmem or 16 * MIB),
        cost_estimate=pl.CostEstimate(flops=flops, bytes_accessed=moved, transcendentals=0),
    )


def shift_z(v, d):
    pairs = [(z * NX + x, ((z + d) % NZ) * NX + x) for z in range(NZ) for x in range(NX)]
    return lax.ppermute(v, "dp", pairs)


def shift_x(v, k):
    pairs = [(z * NX + x, z * NX + (x + k) % NX) for z in range(NZ) for x in range(NX)]
    return lax.ppermute(v, "dp", pairs)


def exchange(v):
    v = v.reshape(FLIGHT, CAP, 2 * D)
    return lax.all_to_all(v, "expert", split_axis=0, concat_axis=0, tiled=True).reshape(ROWS, 2 * D)


def on_device(tokens, route_ids, route_weights, upstream, w_gate, w_up, w_down):
    ids_t, weights_t = route_ids.T, route_weights.T
    shard = call(pack_kernel, [((SH, PW), BF)])(w_gate[0], w_up[0], w_down[0])
    block = jnp.concatenate([shard] + [shift_z(shard, d) for d in range(1, NZ)], axis=0)
    sent = call(dispatch_kernel, [((ROWS, 2 * D), BF)], flops=4 * ROWS * TOK * D)(
        ids_t, weights_t, tokens, upstream
    )
    recv = exchange(sent)
    blocks = [block] + [shift_x(block, k) for k in range(1, NX)]
    quarter = ((NZ * SH, PW), BF)
    back, *quarters = call(
        expert_kernel,
        [((ROWS, 2 * D), BF)] + [quarter] * NX,
        scratch=[pltpu.VMEM((D, PW), BF), pltpu.VMEM((D, PW), BF)],
        vmem=40 * MIB,
        flops=18 * ROWS * D * FF,
        moved=8 * MIB,
    )(recv, *blocks)
    home = exchange(back)
    arrived = [quarters[0]] + [shift_x(quarters[k], k) for k in range(1, NX)]
    slices = call(sum_x_kernel, [((SH, PW), BF)] * NZ, moved=4 * MIB)(*arrived)
    parts = [slices[0]] + [shift_z(slices[d], d) for d in range(1, NZ)]
    grad_gate, grad_up, grad_down = call(
        sum_z_kernel, [((SH, FF), BF), ((SH, FF), BF), ((FD, D), BF)]
    )(*parts)
    mixed, grad_tokens, grad_route = call(
        combine_kernel,
        [((TOK, D), BF), ((TOK, D), BF), ((8, TOK), F32)],
        flops=4 * ROWS * TOK * D,
        moved=2 * MIB,
    )(ids_t, weights_t, upstream, home)
    return (mixed, grad_tokens, grad_route.T, grad_gate[None], grad_up[None], grad_down[None])


def solution(mesh):
    rows, held = P(("dp", "expert"), None), P("expert", "dp", None)
    return jax.shard_map(
        on_device,
        mesh=mesh,
        in_specs=(rows, rows, rows, rows, held, held, held),
        out_specs=(rows, rows, rows, held, held, held),
        check_vma=False,
    )
```

```python
import jax
import jax.numpy as jnp
from jax import lax
from jax.experimental import pallas as pl
from jax.experimental.pallas import tpu as pltpu
from jax.sharding import PartitionSpec as P

FLIGHT = 16
CAP = 16
NZ = 8
NX = 4
TOK = 128
D = 1024
FF = 384
ROWS = FLIGHT * CAP
FD = FF // (NZ * NX)
SH = D // (NZ * NX)
PW = 2 * FF + D // 2
BF = jnp.bfloat16
F32 = jnp.float32
MIB = 1 << 20


def dot(a, b, dims):
    return lax.dot_general(a, b, (dims, ((), ())), preferred_element_type=F32)


def nn(a, b):
    return dot(a, b, ((1,), (0,)))


def tn(a, b):
    return dot(a, b, ((0,), (0,)))


def nt(a, b):
    return dot(a, b, ((1,), (1,)))


def route_rows(ids_t, weights_t):
    live = ids_t < FLIGHT
    expert = jnp.sum(jnp.where(live, ids_t, 0), axis=0, keepdims=True)
    weight = jnp.sum(jnp.where(live, weights_t, 0.0), axis=0, keepdims=True)
    alive = jnp.max(live.astype(jnp.int32), axis=0, keepdims=True) > 0
    return live, expert, weight, alive


def place(ids_t, weights_t):
    live, expert, weight, alive = route_rows(ids_t, weights_t)
    named = (lax.broadcasted_iota(jnp.int32, (FLIGHT, TOK), 0) == expert) & alive
    before = lax.broadcasted_iota(jnp.int32, (TOK, TOK), 0) < lax.broadcasted_iota(
        jnp.int32, (TOK, TOK), 1
    )
    rank = nn(named.astype(F32).astype(BF), before.astype(F32).astype(BF))
    slot = jnp.sum(jnp.where(named, rank, 0.0), axis=0, keepdims=True).astype(jnp.int32)
    row = jnp.where(alive, expert * CAP + slot, -1)
    mask = lax.broadcasted_iota(jnp.int32, (ROWS, TOK), 0) == row
    return live, weight, mask


def column_of(row):
    eye = lax.broadcasted_iota(jnp.int32, (TOK, TOK), 0) == lax.broadcasted_iota(
        jnp.int32, (TOK, TOK), 1
    )
    return jnp.sum(jnp.where(eye, row, 0.0), axis=1, keepdims=True)


def row_of(column):
    eye = lax.broadcasted_iota(jnp.int32, (TOK, TOK), 0) == lax.broadcasted_iota(
        jnp.int32, (TOK, TOK), 1
    )
    return jnp.sum(jnp.where(eye, column, 0.0), axis=0, keepdims=True)


def pack_kernel(gate_ref, up_ref, down_ref, out_ref, gate, up, sems):
    copies = [
        pltpu.make_async_copy(gate_ref, gate, sems.at[0]),
        pltpu.make_async_copy(up_ref, up, sems.at[1]),
    ]
    for copy in copies:
        copy.start()
    down = jnp.concatenate(
        [down_ref[...].astype(F32), jnp.zeros((16 - FD, D), F32)], axis=0
    ).astype(BF)
    for i in range(NZ):
        out_ref[i, :16, 2 * FF :] = down[:, : D // 2]
        out_ref[i, 16:, 2 * FF :] = down[:, D // 2 :]
    for copy in copies:
        copy.wait()
    for i in range(NZ):
        out_ref[i, :, :FF] = gate[...]
        out_ref[i, :, FF : 2 * FF] = up[...]


def dispatch_kernel(ids_ref, weights_ref, tokens_ref, upstream_ref, out_ref):
    live, weight, mask = place(ids_ref[...], weights_ref[...])
    picker = mask.astype(F32).astype(BF)
    out_ref[:, :D] = nn(picker, tokens_ref[...]).astype(BF)
    row_weight = jnp.sum(jnp.where(mask, weight, 0.0), axis=1, keepdims=True)
    out_ref[:, D:] = (row_weight * nn(picker, upstream_ref[...])).astype(BF)


def expert_kernel(*refs):
    recv_ref, weights_ref = refs[:2]
    (sent_ref, q_own, q_right_lo, q_right_hi, q_left_lo, q_left_hi, q_far_lo, q_far_hi) = refs[2:10]
    recv, sent, full, grads, sems = refs[10:]
    x = lax.axis_index("dp") % NX
    to_right, to_left, across = (lax.rem(x + k, NX) for k in (1, NX - 1, 2))
    low, high = pl.ds(0, NZ // 2), pl.ds(NZ // 2, NZ // 2)
    every = pl.ds(0, NZ)

    def spots(buffer):
        return (
            buffer.at[every, x],
            buffer.at[low, to_left],
            buffer.at[high, to_right],
            buffer.at[high, to_left],
            buffer.at[low, to_right],
            buffer.at[low, across],
            buffer.at[high, across],
        )

    starts = [0] + [NZ + i * (NZ // 2) for i in range(7)]
    pieces = [weights_ref.at[pl.ds(a, b - a)] for a, b in zip(starts[:-1], starts[1:])]
    fetches = [pltpu.make_async_copy(recv_ref, recv, sems.at[0])]
    for i, (piece, spot) in enumerate(zip(pieces, spots(full))):
        fetches.append(pltpu.make_async_copy(piece, spot, sems.at[1 + i]))
    for fetch in fetches:
        fetch.start()
    column = lax.broadcasted_iota(jnp.int32, (FF, 16 * NZ * NX), 1)
    of_row = (column // 16) * FD + column % 16
    row = lax.broadcasted_iota(jnp.int32, (FF, 16 * NZ * NX), 0)
    unpad = ((row == of_row) & (column % 16 < FD)).astype(F32).astype(BF)
    for fetch in fetches:
        fetch.wait()

    gate = full[:, :, :, :FF].reshape(D, FF)
    up = full[:, :, :, FF : 2 * FF].reshape(D, FF)
    upper = full[:, :, :16, 2 * FF :].reshape(16 * NZ * NX, D // 2)
    lower = full[:, :, 16:, 2 * FF :].reshape(16 * NZ * NX, D // 2)
    down = jnp.concatenate([nn(unpad, upper).astype(BF), nn(unpad, lower).astype(BF)], axis=1)
    rows, scaled = recv[:, :D], recv[:, D:]
    pre_gate = nn(rows, gate)
    pre_up = nn(rows, up)
    grad_hidden = nt(scaled, down)
    sigma = jax.nn.sigmoid(pre_gate)
    silu = pre_gate * sigma
    hidden = (silu * pre_up).astype(BF)
    sent[:, :D] = nn(hidden, down).astype(BF)
    grad_gate_pre = (grad_hidden * pre_up * sigma * (1.0 + pre_gate * (1.0 - sigma))).astype(BF)
    grad_up_pre = (grad_hidden * silu).astype(BF)
    sent[:, D:] = (nt(grad_gate_pre, gate) + nt(grad_up_pre, up)).astype(BF)
    stores = [pltpu.make_async_copy(sent, sent_ref, sems.at[0])]
    stores[0].start()
    grads[:, :, :, :FF] = tn(rows, grad_gate_pre).astype(BF).reshape(NZ, NX, SH, FF)
    grads[:, :, :, FF : 2 * FF] = tn(rows, grad_up_pre).astype(BF).reshape(NZ, NX, SH, FF)
    hidden_padded = nn(hidden, unpad).astype(BF)
    part_down = tn(hidden_padded, scaled).astype(BF)
    grads[:, :, :16, 2 * FF :] = part_down[:, : D // 2].reshape(NZ, NX, 16, D // 2)
    grads[:, :, 16:, 2 * FF :] = part_down[:, D // 2 :].reshape(NZ, NX, 16, D // 2)
    pieces = (q_own, q_left_lo, q_right_hi, q_left_hi, q_right_lo, q_far_lo, q_far_hi)
    for i, (piece, spot) in enumerate(zip(pieces, spots(grads))):
        stores.append(pltpu.make_async_copy(spot, piece, sems.at[1 + i]))
        stores[-1].start()
    for store in stores:
        store.wait()


def add_far_kernel(right_ref, left_ref, low_ref, high_ref, to_right_ref, to_left_ref):
    to_right_ref[...] = (right_ref[...].astype(F32) + low_ref[...].astype(F32)).astype(BF)
    to_left_ref[...] = (left_ref[...].astype(F32) + high_ref[...].astype(F32)).astype(BF)


def sum_x_kernel(own_ref, left_lo, left_hi, right_lo, right_hi, after_ref, out_ref):
    del after_ref
    h = NZ // 2
    low = left_lo[...].astype(F32) + right_lo[...].astype(F32)
    out_ref[:h] = (own_ref[:h].astype(F32) + low).astype(BF)
    high = left_hi[...].astype(F32) + right_hi[...].astype(F32)
    out_ref[h:] = (own_ref[h:].astype(F32) + high).astype(BF)


def sum_z_kernel(parts_ref, gate_ref, up_ref, down_ref):
    total = parts_ref[0].astype(F32)
    for z in range(1, NZ):
        total = total + parts_ref[z].astype(F32)
    gate_ref[...] = total[:, :FF].astype(BF)
    up_ref[...] = total[:, FF : 2 * FF].astype(BF)
    down_ref[:, : D // 2] = total[:FD, 2 * FF :].astype(BF)
    down_ref[:, D // 2 :] = total[16 : 16 + FD, 2 * FF :].astype(BF)


def combine_kernel(ids_ref, weights_ref, upstream_ref, home_ref, mixed_ref, tokens_ref, route_ref):
    live, weight, mask = place(ids_ref[...], weights_ref[...])
    picker = mask.astype(F32).astype(BF)
    tokens_ref[...] = tn(picker, home_ref[:, D:]).astype(BF)
    picked = tn(picker, home_ref[:, :D])
    mixed_ref[...] = (column_of(weight) * picked).astype(BF)
    inner = jnp.sum(upstream_ref[...].astype(F32) * picked, axis=1, keepdims=True)
    route_ref[...] = jnp.where(live, row_of(inner), 0.0)


def call(kernel, outs, scratch=(), vmem=16 * MIB, flops=0, moved=MIB, spaces=None, any_outs=False):
    shapes = [jax.ShapeDtypeStruct(s, t) for s, t in outs]
    single = len(shapes) == 1
    specs = {}
    if spaces is not None:
        specs["in_specs"] = [pl.BlockSpec(memory_space=a or pltpu.VMEM) for a in spaces]
    if any_outs:
        specs["out_specs"] = [pl.BlockSpec(memory_space=pl.ANY)] * len(outs)
    return pl.pallas_call(
        kernel,
        out_shape=shapes[0] if single else shapes,
        scratch_shapes=list(scratch),
        compiler_params=pltpu.CompilerParams(vmem_limit_bytes=vmem),
        cost_estimate=pl.CostEstimate(flops=flops, bytes_accessed=moved, transcendentals=0),
        **specs,
    )


def swap_z(v):
    groups = [[z * NX + x for z in range(NZ)] for x in range(NX)]
    return lax.all_to_all(
        v, "dp", split_axis=0, concat_axis=0, tiled=True, axis_index_groups=groups
    )


def shift_x(v, k):
    pairs = [(z * NX + x, z * NX + (x + k) % NX) for z in range(NZ) for x in range(NX)]
    return lax.ppermute(v, "dp", pairs)


def exchange(v):
    v = v.reshape(FLIGHT, CAP, 2 * D)
    return lax.all_to_all(v, "expert", split_axis=0, concat_axis=0, tiled=True).reshape(ROWS, 2 * D)


def on_device(tokens, route_ids, route_weights, upstream, w_gate, w_up, w_down):
    ids_t, weights_t = route_ids.T, route_weights.T
    shard = pltpu.VMEM((SH, FF), BF)
    copies = call(
        pack_kernel,
        [((NZ, SH, PW), BF)],
        scratch=[shard, shard, pltpu.SemaphoreType.DMA((2,))],
        vmem=58 * MIB,
        spaces=(pl.ANY, pl.ANY, None),
    )(w_gate[0], w_up[0], w_down[0])
    own = swap_z(copies)
    sent = call(dispatch_kernel, [((ROWS, 2 * D), BF)], flops=4 * ROWS * TOK * D)(
        ids_t, weights_t, tokens, upstream
    )
    recv = exchange(sent)
    half = NZ // 2
    low, high = own[:half], own[half:]
    left_lo, right_hi = shift_x(low, 1), shift_x(high, NX - 1)
    left_hi, right_lo = shift_x(high, 1), shift_x(low, NX - 1)
    far_lo, far_hi = shift_x(left_lo, 1), shift_x(right_hi, NX - 1)
    whole, part = ((NZ, SH, PW), BF), ((half, SH, PW), BF)
    tile = pltpu.VMEM((ROWS, 2 * D), BF)
    matrix = pltpu.VMEM((NZ, NX, SH, PW), BF)
    back, q_own, q_right_lo, q_right_hi, q_left_lo, q_left_hi, q_far_lo, q_far_hi = call(
        expert_kernel,
        [((ROWS, 2 * D), BF), whole] + [part] * 6,
        scratch=[tile, tile, matrix, matrix, pltpu.SemaphoreType.DMA((8,))],
        vmem=48 * MIB,
        flops=18 * ROWS * D * FF,
        moved=8 * MIB,
        spaces=(pl.ANY,) * 2,
        any_outs=True,
    )(
        recv,
        jnp.concatenate([own, left_lo, right_hi, left_hi, right_lo, far_lo, far_hi], axis=0),
    )
    home = exchange(back)
    add_lo, add_hi = shift_x(q_far_lo, 1), shift_x(q_far_hi, NX - 1)
    from_left_hi, from_right_lo = shift_x(q_right_hi, 1), shift_x(q_left_lo, NX - 1)
    to_right, to_left = call(add_far_kernel, [part, part], moved=2 * MIB)(
        q_right_lo, q_left_hi, add_lo, add_hi
    )
    from_left_lo, from_right_hi = shift_x(to_right, 1), shift_x(to_left, NX - 1)
    total = call(sum_x_kernel, [whole], moved=3 * MIB, spaces=(None,) * 5 + (pl.ANY,))(
        q_own, from_left_lo, from_left_hi, from_right_lo, from_right_hi, home
    )
    parts = swap_z(total)
    grad_gate, grad_up, grad_down = call(
        sum_z_kernel, [((SH, FF), BF), ((SH, FF), BF), ((FD, D), BF)]
    )(parts)
    mixed, grad_tokens, grad_route = call(
        combine_kernel,
        [((TOK, D), BF), ((TOK, D), BF), ((8, TOK), F32)],
        flops=4 * ROWS * TOK * D,
        moved=2 * MIB,
    )(ids_t, weights_t, upstream, home)
    return (mixed, grad_tokens, grad_route.T, grad_gate[None], grad_up[None], grad_down[None])


def solution(mesh):
    rows, held = P(("dp", "expert"), None), P("expert", "dp", None)
    return jax.shard_map(
        on_device,
        mesh=mesh,
        in_specs=(rows, rows, rows, rows, held, held, held),
        out_specs=(rows, rows, rows, held, held, held),
        check_vma=False,
    )
```

```python
import jax
import jax.numpy as jnp
from jax import lax
from jax.experimental import pallas as pl
from jax.experimental.pallas import tpu as pltpu
from jax.sharding import PartitionSpec as P

FLIGHT = 16
CAP = 16
NZ = 8
NX = 4
TOK = 128
D = 1024
FF = 384
ROWS = FLIGHT * CAP
FD = FF // (NZ * NX)
SH = D // (NZ * NX)
PW = 2 * FF
PH = SH + 16
DN = 16 * NZ * NX
TW = D - PW
STACK = FD // 3
BF = jnp.bfloat16
F32 = jnp.float32
MIB = 1 << 20


def dot(a, b, dims):
    return lax.dot_general(a, b, (dims, ((), ())), preferred_element_type=F32)


def nn(a, b):
    return dot(a, b, ((1,), (0,)))


def tn(a, b):
    return dot(a, b, ((0,), (0,)))


def nt(a, b):
    return dot(a, b, ((1,), (1,)))


def route_rows(ids_t, weights_t):
    live = ids_t < FLIGHT
    expert = jnp.sum(jnp.where(live, ids_t, 0), axis=0, keepdims=True)
    weight = jnp.sum(jnp.where(live, weights_t, 0.0), axis=0, keepdims=True)
    alive = jnp.max(live.astype(jnp.int32), axis=0, keepdims=True) > 0
    return live, expert, weight, alive


def place(ids_t, weights_t):
    live, expert, weight, alive = route_rows(ids_t, weights_t)
    named = (lax.broadcasted_iota(jnp.int32, (FLIGHT, TOK), 0) == expert) & alive
    before = lax.broadcasted_iota(jnp.int32, (TOK, TOK), 0) < lax.broadcasted_iota(
        jnp.int32, (TOK, TOK), 1
    )
    rank = nn(named.astype(F32).astype(BF), before.astype(F32).astype(BF))
    slot = jnp.sum(jnp.where(named, rank, 0.0), axis=0, keepdims=True).astype(jnp.int32)
    core = lax.axis_index("expert") % 2
    row = jnp.where(expert % 2 == core, 0, ROWS // 2) + (expert // 2) * CAP + slot
    mask = lax.broadcasted_iota(jnp.int32, (ROWS, TOK), 0) == jnp.where(alive, row, -1)
    return live, weight, mask


def column_of(row):
    eye = lax.broadcasted_iota(jnp.int32, (TOK, TOK), 0) == lax.broadcasted_iota(
        jnp.int32, (TOK, TOK), 1
    )
    return jnp.sum(jnp.where(eye, row, 0.0), axis=1, keepdims=True)


def row_of(column):
    eye = lax.broadcasted_iota(jnp.int32, (TOK, TOK), 0) == lax.broadcasted_iota(
        jnp.int32, (TOK, TOK), 1
    )
    return jnp.sum(jnp.where(eye, column, 0.0), axis=0, keepdims=True)


def pack_kernel(gate_ref, up_ref, down_ref, out_ref, gate, up, sems):
    copies = [
        pltpu.make_async_copy(gate_ref, gate, sems.at[0]),
        pltpu.make_async_copy(up_ref, up, sems.at[1]),
    ]
    for copy in copies:
        copy.start()
    down = down_ref[...].astype(F32)
    tail = [down[i * STACK : (i + 1) * STACK, PW:] for i in range(3)]
    packed = jnp.concatenate([down[:, :PW], jnp.concatenate(tail, axis=1)], axis=0)
    for i in range(NZ):
        out_ref[i, SH:, :] = packed.astype(BF)
    for copy in copies:
        copy.wait()
    for i in range(NZ):
        out_ref[i, :SH, :FF] = gate[...]
        out_ref[i, :SH, FF:] = up[...]


def unpad_matrices():
    f = lax.broadcasted_iota(jnp.int32, (FF, DN), 0)
    j = lax.broadcasted_iota(jnp.int32, (FF, DN), 1)
    base = (f // FD) * 16
    r = f % FD
    body = (j == base + r).astype(F32).astype(BF)
    tails = []
    for i in range(3):
        here = (r // STACK == i) & (j == base + FD + r % STACK)
        tails.append(here.astype(F32).astype(BF))
    return body, tails


def dispatch_kernel(ids_ref, weights_ref, tokens_ref, upstream_ref, keep_ref, give_ref):
    live, weight, mask = place(ids_ref[...], weights_ref[...])
    picker = mask.astype(F32).astype(BF)
    row_weight = jnp.sum(jnp.where(mask, weight, 0.0), axis=1, keepdims=True)
    rows = nn(picker, tokens_ref[...]).astype(BF)
    scaled = (row_weight * nn(picker, upstream_ref[...])).astype(BF)
    keep_ref[:, :D] = rows[: ROWS // 2]
    keep_ref[:, D:] = scaled[: ROWS // 2]
    give_ref[:, :D] = rows[ROWS // 2 :]
    give_ref[:, D:] = scaled[ROWS // 2 :]


def merge_kernel(keep_ref, got_ref, out_ref, sems):
    core = lax.axis_index("expert") % 2
    copies = [
        pltpu.make_async_copy(keep_ref, out_ref.at[:, core], sems.at[0]),
        pltpu.make_async_copy(got_ref, out_ref.at[:, 1 - core], sems.at[1]),
    ]
    for copy in copies:
        copy.start()
    for copy in copies:
        copy.wait()


def give_kernel(home_ref, after_ref, give_ref, sem):
    del after_ref
    core = lax.axis_index("expert") % 2
    copy = pltpu.make_async_copy(home_ref.at[:, 1 - core], give_ref, sem)
    copy.start()
    copy.wait()


def expert_kernel(*refs):
    recv_ref, weights_ref = refs[:2]
    (sent_ref, q_own, q_right_lo, q_right_hi, q_left_lo, q_left_hi, q_far_lo, q_far_hi) = refs[2:10]
    recv, sent, full, grads, sems = refs[10:]
    x = lax.axis_index("dp") % NX
    to_right, to_left, across = (lax.rem(x + k, NX) for k in (1, NX - 1, 2))
    low, high = pl.ds(0, NZ // 2), pl.ds(NZ // 2, NZ // 2)
    every = pl.ds(0, NZ)

    def spots(buffer):
        return (
            buffer.at[every, x],
            buffer.at[low, to_left],
            buffer.at[high, to_right],
            buffer.at[high, to_left],
            buffer.at[low, to_right],
            buffer.at[low, across],
            buffer.at[high, across],
        )

    starts = [0] + [NZ + i * (NZ // 2) for i in range(7)]
    pieces = [weights_ref.at[pl.ds(a, b - a)] for a, b in zip(starts[:-1], starts[1:])]
    fetches = [pltpu.make_async_copy(recv_ref, recv, sems.at[0])]
    for i, (piece, spot) in enumerate(zip(pieces, spots(full))):
        fetches.append(pltpu.make_async_copy(piece, spot, sems.at[1 + i]))
    for fetch in fetches:
        fetch.start()
    body, tails = unpad_matrices()
    for fetch in fetches:
        fetch.wait()

    gate = full[:, :, :SH, :FF].reshape(D, FF)
    up = full[:, :, :SH, FF:].reshape(D, FF)
    packed = full[:, :, SH:, :].reshape(DN, PW)
    last = sum(nn(tails[i], packed[:, i * TW : (i + 1) * TW]) for i in range(3))
    down = jnp.concatenate([nn(body, packed).astype(BF), last.astype(BF)], axis=1)
    rows, scaled = recv[:, :D], recv[:, D:]
    pre_gate = nn(rows, gate)
    pre_up = nn(rows, up)
    grad_hidden = nt(scaled, down)
    sigma = jax.nn.sigmoid(pre_gate)
    silu = pre_gate * sigma
    hidden = (silu * pre_up).astype(BF)
    sent[:, :D] = nn(hidden, down).astype(BF)
    grad_gate_pre = (grad_hidden * pre_up * sigma * (1.0 + pre_gate * (1.0 - sigma))).astype(BF)
    grad_up_pre = (grad_hidden * silu).astype(BF)
    sent[:, D:] = (nt(grad_gate_pre, gate) + nt(grad_up_pre, up)).astype(BF)
    stores = [pltpu.make_async_copy(sent, sent_ref, sems.at[0])]
    stores[0].start()
    grads[:, :, :SH, :FF] = tn(rows, grad_gate_pre).astype(BF).reshape(NZ, NX, SH, FF)
    grads[:, :, :SH, FF:] = tn(rows, grad_up_pre).astype(BF).reshape(NZ, NX, SH, FF)
    hidden_body = nn(hidden, body).astype(BF)
    for i in range(3):
        cols = slice(i * TW, (i + 1) * TW)
        part = tn(hidden_body, scaled[:, cols]) + tn(nn(hidden, tails[i]).astype(BF), scaled[:, PW:])
        grads[:, :, SH:, cols] = part.astype(BF).reshape(NZ, NX, 16, TW)
    pieces = (q_own, q_left_lo, q_right_hi, q_left_hi, q_right_lo, q_far_lo, q_far_hi)
    for i, (piece, spot) in enumerate(zip(pieces, spots(grads))):
        stores.append(pltpu.make_async_copy(spot, piece, sems.at[1 + i]))
        stores[-1].start()
    for store in stores:
        store.wait()


def add_far_kernel(right_ref, left_ref, low_ref, high_ref, to_right_ref, to_left_ref):
    to_right_ref[...] = (right_ref[...].astype(F32) + low_ref[...].astype(F32)).astype(BF)
    to_left_ref[...] = (left_ref[...].astype(F32) + high_ref[...].astype(F32)).astype(BF)


def sum_x_kernel(own_ref, left_lo, left_hi, right_lo, right_hi, after_ref, out_ref):
    del after_ref
    h = NZ // 2
    low = left_lo[...].astype(F32) + right_lo[...].astype(F32)
    out_ref[:h] = (own_ref[:h].astype(F32) + low).astype(BF)
    high = left_hi[...].astype(F32) + right_hi[...].astype(F32)
    out_ref[h:] = (own_ref[h:].astype(F32) + high).astype(BF)


def sum_z_kernel(parts_ref, gate_ref, up_ref, down_ref):
    total = parts_ref[0].astype(F32)
    for z in range(1, NZ):
        total = total + parts_ref[z].astype(F32)
    gate_ref[...] = total[:SH, :FF].astype(BF)
    up_ref[...] = total[:SH, FF:].astype(BF)
    tail = [total[SH + FD :, i * TW : (i + 1) * TW] for i in range(3)]
    down_ref[:, :PW] = total[SH : SH + FD, :].astype(BF)
    down_ref[:, PW:] = jnp.concatenate(tail, axis=0).astype(BF)


def combine_kernel(
    ids_ref, weights_ref, upstream_ref, home_ref, got_ref, mixed_ref, tokens_ref, route_ref, rows, sems
):
    core = lax.axis_index("expert") % 2
    copies = [
        pltpu.make_async_copy(home_ref.at[:, core], rows.at[0], sems.at[0]),
        pltpu.make_async_copy(got_ref, rows.at[1], sems.at[1]),
    ]
    for copy in copies:
        copy.start()
    live, weight, mask = place(ids_ref[...], weights_ref[...])
    picker = mask.astype(F32).astype(BF)
    for copy in copies:
        copy.wait()
    home = rows[...].reshape(ROWS, 2 * D)
    tokens_ref[...] = tn(picker, home[:, D:]).astype(BF)
    picked = tn(picker, home[:, :D])
    mixed_ref[...] = (column_of(weight) * picked).astype(BF)
    inner = jnp.sum(upstream_ref[...].astype(F32) * picked, axis=1, keepdims=True)
    route_ref[...] = jnp.where(live, row_of(inner), 0.0)


def call(kernel, outs, scratch=(), vmem=16 * MIB, flops=0, moved=MIB, spaces=None, out_spaces=None):
    shapes = [jax.ShapeDtypeStruct(s, t) for s, t in outs]
    single = len(shapes) == 1
    specs = {}
    if spaces is not None:
        specs["in_specs"] = [pl.BlockSpec(memory_space=a or pltpu.VMEM) for a in spaces]
    if out_spaces is not None:
        specs["out_specs"] = [pl.BlockSpec(memory_space=a) for a in out_spaces]
        if single:
            specs["out_specs"] = specs["out_specs"][0]
    return pl.pallas_call(
        kernel,
        out_shape=shapes[0] if single else shapes,
        scratch_shapes=list(scratch),
        compiler_params=pltpu.CompilerParams(vmem_limit_bytes=vmem),
        cost_estimate=pl.CostEstimate(flops=flops, bytes_accessed=moved, transcendentals=0),
        **specs,
    )


Z_GROUPS = [[z * NX + x for z in range(NZ)] for x in range(NX)]


def swap_z(v):
    return lax.all_to_all(
        v, "dp", split_axis=0, concat_axis=0, tiled=True, axis_index_groups=Z_GROUPS
    )


def shift_x(v, k):
    pairs = [(z * NX + x, z * NX + (x + k) % NX) for z in range(NZ) for x in range(NX)]
    return lax.ppermute(v, "dp", pairs)


NY = FLIGHT // 2
Y_GROUPS = [[2 * y + core for y in range(NY)] for core in range(2)]


def swap_core(v):
    return lax.ppermute(v, "expert", [(i, i ^ 1) for i in range(FLIGHT)])


def exchange(v):
    return lax.all_to_all(
        v, "expert", split_axis=0, concat_axis=0, tiled=True, axis_index_groups=Y_GROUPS
    )


def on_device(tokens, route_ids, route_weights, upstream, w_gate, w_up, w_down):
    ids_t, weights_t = route_ids.T, route_weights.T
    held = pltpu.VMEM((SH, FF), BF)
    copies = call(
        pack_kernel,
        [((NZ, PH, PW), BF)],
        scratch=[held, held, pltpu.SemaphoreType.DMA((2,))],
        vmem=58 * MIB,
        spaces=(pl.ANY, pl.ANY, None),
    )(w_gate[0], w_up[0], w_down[0])
    both, one = ((NY, 2, CAP, 2 * D), BF), ((NY, CAP, 2 * D), BF)
    keep, give = call(
        dispatch_kernel, [((ROWS // 2, 2 * D), BF)] * 2, vmem=58 * MIB, flops=4 * ROWS * TOK * D
    )(ids_t, weights_t, tokens, upstream)
    sent = call(
        merge_kernel,
        [both],
        scratch=[pltpu.SemaphoreType.DMA((2,))],
        spaces=(pl.ANY, pl.ANY),
        out_spaces=(pl.ANY,),
    )(keep.reshape(one[0]), swap_core(give).reshape(one[0]))
    own = swap_z(copies)
    recv = exchange(sent).reshape(ROWS, 2 * D)
    half = NZ // 2
    low, high = own[:half], own[half:]
    left_lo, right_hi = shift_x(low, 1), shift_x(high, NX - 1)
    left_hi, right_lo = shift_x(high, 1), shift_x(low, NX - 1)
    far_lo, far_hi = shift_x(left_lo, 1), shift_x(right_hi, NX - 1)
    whole, part = ((NZ, PH, PW), BF), ((half, PH, PW), BF)
    tile = pltpu.VMEM((ROWS, 2 * D), BF)
    matrix = pltpu.VMEM((NZ, NX, PH, PW), BF)
    back, q_own, q_right_lo, q_right_hi, q_left_lo, q_left_hi, q_far_lo, q_far_hi = call(
        expert_kernel,
        [((ROWS, 2 * D), BF), whole] + [part] * 6,
        scratch=[tile, tile, matrix, matrix, pltpu.SemaphoreType.DMA((8,))],
        vmem=48 * MIB,
        flops=18 * ROWS * D * FF,
        moved=8 * MIB,
        spaces=(pl.ANY,) * 2,
        out_spaces=(pl.ANY,) * 8,
    )(
        recv,
        jnp.concatenate([own, left_lo, right_hi, left_hi, right_lo, far_lo, far_hi], axis=0),
    )
    home = exchange(back.reshape(both[0]))
    add_lo, add_hi = shift_x(q_far_lo, 1), shift_x(q_far_hi, NX - 1)
    from_left_hi, from_right_lo = shift_x(q_right_hi, 1), shift_x(q_left_lo, NX - 1)
    to_right, to_left = call(add_far_kernel, [part, part], moved=2 * MIB)(
        q_right_lo, q_left_hi, add_lo, add_hi
    )
    from_left_lo, from_right_hi = shift_x(to_right, 1), shift_x(to_left, NX - 1)
    total = call(sum_x_kernel, [whole], moved=3 * MIB, spaces=(None,) * 5 + (pl.ANY,))(
        q_own, from_left_lo, from_left_hi, from_right_lo, from_right_hi, home
    )
    got = swap_core(
        call(
            give_kernel,
            [one],
            scratch=[pltpu.SemaphoreType.DMA],
            spaces=(pl.ANY, pl.ANY),
            out_spaces=(pl.ANY,),
        )(home, total)
    )
    parts = swap_z(total)
    grad_gate, grad_up, grad_down = call(
        sum_z_kernel, [((SH, FF), BF), ((SH, FF), BF), ((FD, D), BF)]
    )(parts)
    mixed, grad_tokens, grad_route = call(
        combine_kernel,
        [((TOK, D), BF), ((TOK, D), BF), ((8, TOK), F32)],
        scratch=[pltpu.VMEM((2,) + one[0], BF), pltpu.SemaphoreType.DMA((2,))],
        flops=4 * ROWS * TOK * D,
        moved=2 * MIB,
        spaces=(None, None, None, pl.ANY, pl.ANY),
    )(ids_t, weights_t, upstream, home, got)
    return (mixed, grad_tokens, grad_route.T, grad_gate[None], grad_up[None], grad_down[None])


def solution(mesh):
    rows, held = P(("dp", "expert"), None), P("expert", "dp", None)
    return jax.shard_map(
        on_device,
        mesh=mesh,
        in_specs=(rows, rows, rows, rows, held, held, held),
        out_specs=(rows, rows, rows, held, held, held),
        check_vma=False,
    )
```

```python
import jax
import jax.numpy as jnp
from jax import lax
from jax.experimental import pallas as pl
from jax.experimental.pallas import tpu as pltpu
from jax.sharding import PartitionSpec as P

FLIGHT = 16
CAP = 16
NZ = 8
NX = 4
TOK = 128
D = 1024
FF = 384
ROWS = FLIGHT * CAP
FD = FF // (NZ * NX)
SH = D // (NZ * NX)
PW = 2 * FF
PH = SH + 16
TW = D - PW
STACK = FD // 3
BF = jnp.bfloat16
F32 = jnp.float32
MIB = 1 << 20


def dot(a, b, dims):
    return lax.dot_general(a, b, (dims, ((), ())), preferred_element_type=F32)


def nn(a, b):
    return dot(a, b, ((1,), (0,)))


def tn(a, b):
    return dot(a, b, ((0,), (0,)))


def nt(a, b):
    return dot(a, b, ((1,), (1,)))


def route_rows(ids_t, weights_t):
    live = ids_t < FLIGHT
    expert = jnp.sum(jnp.where(live, ids_t, 0), axis=0, keepdims=True)
    weight = jnp.sum(jnp.where(live, weights_t, 0.0), axis=0, keepdims=True)
    alive = jnp.max(live.astype(jnp.int32), axis=0, keepdims=True) > 0
    return live, expert, weight, alive


def place(ids_t, weights_t):
    live, expert, weight, alive = route_rows(ids_t, weights_t)
    named = (lax.broadcasted_iota(jnp.int32, (FLIGHT, TOK), 0) == expert) & alive
    before = lax.broadcasted_iota(jnp.int32, (TOK, TOK), 0) < lax.broadcasted_iota(
        jnp.int32, (TOK, TOK), 1
    )
    rank = nn(named.astype(F32).astype(BF), before.astype(F32).astype(BF))
    slot = jnp.sum(jnp.where(named, rank, 0.0), axis=0, keepdims=True).astype(jnp.int32)
    core = lax.axis_index("expert") % 2
    row = jnp.where(expert % 2 == core, 0, ROWS // 2) + (expert // 2) * CAP + slot
    mask = lax.broadcasted_iota(jnp.int32, (ROWS, TOK), 0) == jnp.where(alive, row, -1)
    return live, weight, mask


def column_of(row):
    eye = lax.broadcasted_iota(jnp.int32, (TOK, TOK), 0) == lax.broadcasted_iota(
        jnp.int32, (TOK, TOK), 1
    )
    return jnp.sum(jnp.where(eye, row, 0.0), axis=1, keepdims=True)


def row_of(column):
    eye = lax.broadcasted_iota(jnp.int32, (TOK, TOK), 0) == lax.broadcasted_iota(
        jnp.int32, (TOK, TOK), 1
    )
    return jnp.sum(jnp.where(eye, column, 0.0), axis=0, keepdims=True)


def pack_kernel(gate_ref, up_ref, down_ref, out_ref):
    down = down_ref[...].astype(F32)
    tail = [down[i * STACK : (i + 1) * STACK, PW:] for i in range(3)]
    packed = jnp.concatenate([down[:, :PW], jnp.concatenate(tail, axis=1)], axis=0).astype(BF)
    for i in range(NZ):
        out_ref[i, SH:, :] = packed
        out_ref[i, :SH, :FF] = gate_ref[...]
        out_ref[i, :SH, FF:] = up_ref[...]


def unpack_down(full, wide):
    for p in range(NZ * NX):
        block = full[p // NX, p % NX, SH:, :].astype(F32)
        wide[p * FD : (p + 1) * FD, :PW] = block[:FD]
        for i in range(3):
            at = p * FD + i * STACK
            wide[at : at + STACK, PW:] = block[FD:, i * TW : (i + 1) * TW]


def pack_down(wide, grads):
    for p in range(NZ * NX):
        at = p * FD
        tail = [wide[at + i * STACK : at + (i + 1) * STACK, PW:] for i in range(3)]
        rows = jnp.concatenate([wide[at : at + FD, :PW], jnp.concatenate(tail, axis=1)], axis=0)
        grads[p // NX, p % NX, SH:, :] = rows.astype(BF)


def dispatch_kernel(ids_ref, weights_ref, tokens_ref, upstream_ref, keep_ref, give_ref):
    live, weight, mask = place(ids_ref[...], weights_ref[...])
    picker = mask.astype(F32).astype(BF)
    row_weight = jnp.sum(jnp.where(mask, weight, 0.0), axis=1, keepdims=True)
    rows = nn(picker, tokens_ref[...]).astype(BF)
    scaled = (row_weight * nn(picker, upstream_ref[...])).astype(BF)
    keep_ref[:, :D] = rows[: ROWS // 2]
    keep_ref[:, D:] = scaled[: ROWS // 2]
    give_ref[:, :D] = rows[ROWS // 2 :]
    give_ref[:, D:] = scaled[ROWS // 2 :]


def merge_kernel(keep_ref, got_ref, out_ref, sems):
    core = lax.axis_index("expert") % 2
    copies = [
        pltpu.make_async_copy(keep_ref, out_ref.at[:, core], sems.at[0]),
        pltpu.make_async_copy(got_ref, out_ref.at[:, 1 - core], sems.at[1]),
    ]
    for copy in copies:
        copy.start()
    for copy in copies:
        copy.wait()


def give_kernel(home_ref, after_ref, give_ref, sem):
    del after_ref
    core = lax.axis_index("expert") % 2
    copy = pltpu.make_async_copy(home_ref.at[:, 1 - core], give_ref, sem)
    copy.start()
    copy.wait()


def expert_kernel(*refs):
    recv_ref, near_ref, *far_refs = refs[:4]
    (sent_ref, q_own, q_right_lo, q_right_hi, q_left_lo, q_left_hi, q_far_lo, q_far_hi) = refs[4:12]
    recv, sent, full, grads, wide, sems = refs[12:]
    x = lax.axis_index("dp") % NX
    to_right, to_left, across = (lax.rem(x + k, NX) for k in (1, NX - 1, 2))
    low, high = pl.ds(0, NZ // 2), pl.ds(NZ // 2, NZ // 2)
    every = pl.ds(0, NZ)

    def spots(buffer):
        return (
            buffer.at[every, x],
            buffer.at[low, to_left],
            buffer.at[high, to_right],
            buffer.at[high, to_left],
            buffer.at[low, to_right],
            buffer.at[low, across],
            buffer.at[high, across],
        )

    starts = [0] + [NZ + i * (NZ // 2) for i in range(5)]
    pieces = [near_ref.at[pl.ds(a, b - a)] for a, b in zip(starts[:-1], starts[1:])] + far_refs
    fetches = [pltpu.make_async_copy(recv_ref, recv, sems.at[0])]
    for i, (piece, spot) in enumerate(zip(pieces, spots(full))):
        fetches.append(pltpu.make_async_copy(piece, spot, sems.at[1 + i]))
    for fetch in fetches:
        fetch.start()
    for fetch in fetches:
        fetch.wait()

    gate = full[:, :, :SH, :FF].reshape(D, FF)
    up = full[:, :, :SH, FF:].reshape(D, FF)
    unpack_down(full, wide)
    down = wide[...].astype(BF)
    rows, scaled = recv[:, :D], recv[:, D:]
    pre_gate = nn(rows, gate)
    pre_up = nn(rows, up)
    grad_hidden = nt(scaled, down)
    sigma = jax.nn.sigmoid(pre_gate)
    silu = pre_gate * sigma
    hidden = (silu * pre_up).astype(BF)
    sent[:, :D] = nn(hidden, down).astype(BF)
    grad_gate_pre = (grad_hidden * pre_up * sigma * (1.0 + pre_gate * (1.0 - sigma))).astype(BF)
    grad_up_pre = (grad_hidden * silu).astype(BF)
    sent[:, D:] = (nt(grad_gate_pre, gate) + nt(grad_up_pre, up)).astype(BF)
    stores = [pltpu.make_async_copy(sent, sent_ref, sems.at[0])]
    stores[0].start()
    grads[:, :, :SH, :FF] = tn(rows, grad_gate_pre).astype(BF).reshape(NZ, NX, SH, FF)
    grads[:, :, :SH, FF:] = tn(rows, grad_up_pre).astype(BF).reshape(NZ, NX, SH, FF)
    wide[...] = tn(hidden, scaled)
    pack_down(wide, grads)
    pieces = (q_own, q_left_lo, q_right_hi, q_left_hi, q_right_lo, q_far_lo, q_far_hi)
    for i, (piece, spot) in enumerate(zip(pieces, spots(grads))):
        stores.append(pltpu.make_async_copy(spot, piece, sems.at[1 + i]))
        stores[-1].start()
    for store in stores:
        store.wait()


def add_far_kernel(right_ref, left_ref, low_ref, high_ref, to_right_ref, to_left_ref):
    to_right_ref[...] = (right_ref[...].astype(F32) + low_ref[...].astype(F32)).astype(BF)
    to_left_ref[...] = (left_ref[...].astype(F32) + high_ref[...].astype(F32)).astype(BF)


def sum_x_kernel(own_ref, left_lo, left_hi, right_lo, right_hi, after_ref, out_ref):
    del after_ref
    h = NZ // 2
    low = left_lo[...].astype(F32) + right_lo[...].astype(F32)
    out_ref[:h] = (own_ref[:h].astype(F32) + low).astype(BF)
    high = left_hi[...].astype(F32) + right_hi[...].astype(F32)
    out_ref[h:] = (own_ref[h:].astype(F32) + high).astype(BF)


def sum_z_kernel(parts_ref, gate_ref, up_ref, down_ref):
    total = parts_ref[0].astype(F32)
    for z in range(1, NZ):
        total = total + parts_ref[z].astype(F32)
    gate_ref[...] = total[:SH, :FF].astype(BF)
    up_ref[...] = total[:SH, FF:].astype(BF)
    tail = [total[SH + FD :, i * TW : (i + 1) * TW] for i in range(3)]
    down_ref[:, :PW] = total[SH : SH + FD, :].astype(BF)
    down_ref[:, PW:] = jnp.concatenate(tail, axis=0).astype(BF)


def combine_kernel(
    ids_ref, weights_ref, upstream_ref, home_ref, got_ref, mixed_ref, tokens_ref, route_ref, rows, sems
):
    core = lax.axis_index("expert") % 2
    copies = [
        pltpu.make_async_copy(home_ref.at[:, core], rows.at[0], sems.at[0]),
        pltpu.make_async_copy(got_ref, rows.at[1], sems.at[1]),
    ]
    for copy in copies:
        copy.start()
    live, weight, mask = place(ids_ref[...], weights_ref[...])
    picker = mask.astype(F32).astype(BF)
    for copy in copies:
        copy.wait()
    home = rows[...].reshape(ROWS, 2 * D)
    tokens_ref[...] = tn(picker, home[:, D:]).astype(BF)
    picked = tn(picker, home[:, :D])
    mixed_ref[...] = (column_of(weight) * picked).astype(BF)
    inner = jnp.sum(upstream_ref[...].astype(F32) * picked, axis=1, keepdims=True)
    route_ref[...] = jnp.where(live, row_of(inner), 0.0)


def call(kernel, outs, scratch=(), vmem=16 * MIB, flops=0, moved=MIB, spaces=None, out_spaces=None):
    shapes = [jax.ShapeDtypeStruct(s, t) for s, t in outs]
    single = len(shapes) == 1
    specs = {}
    if spaces is not None:
        specs["in_specs"] = [pl.BlockSpec(memory_space=a or pltpu.VMEM) for a in spaces]
    if out_spaces is not None:
        specs["out_specs"] = [pl.BlockSpec(memory_space=a) for a in out_spaces]
        if single:
            specs["out_specs"] = specs["out_specs"][0]
    return pl.pallas_call(
        kernel,
        out_shape=shapes[0] if single else shapes,
        scratch_shapes=list(scratch),
        compiler_params=pltpu.CompilerParams(vmem_limit_bytes=vmem),
        cost_estimate=pl.CostEstimate(flops=flops, bytes_accessed=moved, transcendentals=0),
        **specs,
    )


Z_GROUPS = [[z * NX + x for z in range(NZ)] for x in range(NX)]


def swap_z(v):
    return lax.all_to_all(
        v, "dp", split_axis=0, concat_axis=0, tiled=True, axis_index_groups=Z_GROUPS
    )


def shift_x(v, k):
    pairs = [(z * NX + x, z * NX + (x + k) % NX) for z in range(NZ) for x in range(NX)]
    return lax.ppermute(v, "dp", pairs)


NY = FLIGHT // 2
Y_GROUPS = [[2 * y + core for y in range(NY)] for core in range(2)]


def swap_core(v):
    return lax.ppermute(v, "expert", [(i, i ^ 1) for i in range(FLIGHT)])


def exchange(v):
    return lax.all_to_all(
        v, "expert", split_axis=0, concat_axis=0, tiled=True, axis_index_groups=Y_GROUPS
    )


def on_device(tokens, route_ids, route_weights, upstream, w_gate, w_up, w_down):
    ids_t, weights_t = route_ids.T, route_weights.T
    copies = call(pack_kernel, [((NZ, PH, PW), BF)], vmem=58 * MIB)(w_gate[0], w_up[0], w_down[0])
    both, one = ((NY, 2, CAP, 2 * D), BF), ((NY, CAP, 2 * D), BF)
    keep, give = call(
        dispatch_kernel, [((ROWS // 2, 2 * D), BF)] * 2, vmem=58 * MIB, flops=4 * ROWS * TOK * D
    )(ids_t, weights_t, tokens, upstream)
    sent = call(
        merge_kernel,
        [both],
        scratch=[pltpu.SemaphoreType.DMA((2,))],
        spaces=(pl.ANY, pl.ANY),
        out_spaces=(pl.ANY,),
    )(keep.reshape(one[0]), swap_core(give).reshape(one[0]))
    own = swap_z(copies)
    recv = exchange(sent).reshape(ROWS, 2 * D)
    half = NZ // 2
    low, high = own[:half], own[half:]
    left_lo, right_hi = shift_x(low, 1), shift_x(high, NX - 1)
    left_hi, right_lo = shift_x(high, 1), shift_x(low, NX - 1)
    far_lo, far_hi = shift_x(left_lo, 1), shift_x(right_hi, NX - 1)
    whole, part = ((NZ, PH, PW), BF), ((half, PH, PW), BF)
    tile = pltpu.VMEM((ROWS, 2 * D), BF)
    matrix = pltpu.VMEM((NZ, NX, PH, PW), BF)
    back, q_own, q_right_lo, q_right_hi, q_left_lo, q_left_hi, q_far_lo, q_far_hi = call(
        expert_kernel,
        [((ROWS, 2 * D), BF), whole] + [part] * 6,
        scratch=[
            tile,
            tile,
            matrix,
            matrix,
            pltpu.VMEM((FF, D), F32),
            pltpu.SemaphoreType.DMA((8,)),
        ],
        vmem=48 * MIB,
        flops=18 * ROWS * D * FF,
        moved=8 * MIB,
        spaces=(pl.ANY,) * 4,
        out_spaces=(pl.ANY,) * 8,
    )(
        recv,
        jnp.concatenate([own, left_lo, right_hi, left_hi, right_lo], axis=0),
        far_lo,
        far_hi,
    )
    home = exchange(back.reshape(both[0]))
    add_lo, add_hi = shift_x(q_far_lo, 1), shift_x(q_far_hi, NX - 1)
    from_left_hi, from_right_lo = shift_x(q_right_hi, 1), shift_x(q_left_lo, NX - 1)
    to_right, to_left = call(add_far_kernel, [part, part], moved=2 * MIB)(
        q_right_lo, q_left_hi, add_lo, add_hi
    )
    from_left_lo, from_right_hi = shift_x(to_right, 1), shift_x(to_left, NX - 1)
    total = call(sum_x_kernel, [whole], moved=3 * MIB, spaces=(None,) * 5 + (pl.ANY,))(
        q_own, from_left_lo, from_left_hi, from_right_lo, from_right_hi, home
    )
    got = swap_core(
        call(
            give_kernel,
            [one],
            scratch=[pltpu.SemaphoreType.DMA],
            spaces=(pl.ANY, pl.ANY),
            out_spaces=(pl.ANY,),
        )(home, total)
    )
    parts = swap_z(total)
    grad_gate, grad_up, grad_down = call(
        sum_z_kernel, [((SH, FF), BF), ((SH, FF), BF), ((FD, D), BF)]
    )(parts)
    mixed, grad_tokens, grad_route = call(
        combine_kernel,
        [((TOK, D), BF), ((TOK, D), BF), ((8, TOK), F32)],
        scratch=[pltpu.VMEM((2,) + one[0], BF), pltpu.SemaphoreType.DMA((2,))],
        flops=4 * ROWS * TOK * D,
        moved=2 * MIB,
        spaces=(None, None, None, pl.ANY, pl.ANY),
    )(ids_t, weights_t, upstream, home, got)
    return (mixed, grad_tokens, grad_route.T, grad_gate[None], grad_up[None], grad_down[None])


def solution(mesh):
    rows, held = P(("dp", "expert"), None), P("expert", "dp", None)
    return jax.shard_map(
        on_device,
        mesh=mesh,
        in_specs=(rows, rows, rows, rows, held, held, held),
        out_specs=(rows, rows, rows, held, held, held),
        check_vma=False,
    )
```

```python
import jax
import jax.numpy as jnp
from jax import lax
from jax.experimental import pallas as pl
from jax.experimental.pallas import tpu as pltpu
from jax.sharding import PartitionSpec as P

FLIGHT = 16
CAP = 16
NZ = 8
NX = 4
TOK = 128
D = 1024
FF = 384
ROWS = FLIGHT * CAP
FD = FF // (NZ * NX)
SH = D // (NZ * NX)
PW = 2 * FF
PH = SH + 16
TW = D - PW
STACK = FD // 3
LO = 3
BF = jnp.bfloat16
F32 = jnp.float32
MIB = 1 << 20


def dot(a, b, dims):
    return lax.dot_general(a, b, (dims, ((), ())), preferred_element_type=F32)


def nn(a, b):
    return dot(a, b, ((1,), (0,)))


def tn(a, b):
    return dot(a, b, ((0,), (0,)))


def nt(a, b):
    return dot(a, b, ((1,), (1,)))


def route_rows(ids_t, weights_t):
    live = ids_t < FLIGHT
    expert = jnp.sum(jnp.where(live, ids_t, 0), axis=0, keepdims=True)
    weight = jnp.sum(jnp.where(live, weights_t, 0.0), axis=0, keepdims=True)
    alive = jnp.max(live.astype(jnp.int32), axis=0, keepdims=True) > 0
    return live, expert, weight, alive


def place(ids_t, weights_t):
    live, expert, weight, alive = route_rows(ids_t, weights_t)
    named = (lax.broadcasted_iota(jnp.int32, (FLIGHT, TOK), 0) == expert) & alive
    before = lax.broadcasted_iota(jnp.int32, (TOK, TOK), 0) < lax.broadcasted_iota(
        jnp.int32, (TOK, TOK), 1
    )
    rank = nn(named.astype(F32).astype(BF), before.astype(F32).astype(BF))
    slot = jnp.sum(jnp.where(named, rank, 0.0), axis=0, keepdims=True).astype(jnp.int32)
    core = lax.axis_index("expert") % 2
    row = jnp.where(expert % 2 == core, 0, ROWS // 2) + (expert // 2) * CAP + slot
    mask = lax.broadcasted_iota(jnp.int32, (ROWS, TOK), 0) == jnp.where(alive, row, -1)
    return live, weight, mask


def column_of(row):
    eye = lax.broadcasted_iota(jnp.int32, (TOK, TOK), 0) == lax.broadcasted_iota(
        jnp.int32, (TOK, TOK), 1
    )
    return jnp.sum(jnp.where(eye, row, 0.0), axis=1, keepdims=True)


def row_of(column):
    eye = lax.broadcasted_iota(jnp.int32, (TOK, TOK), 0) == lax.broadcasted_iota(
        jnp.int32, (TOK, TOK), 1
    )
    return jnp.sum(jnp.where(eye, column, 0.0), axis=0, keepdims=True)


def pack_kernel(gate_ref, up_ref, down_ref, out_ref):
    down = down_ref[...].astype(F32)
    tail = [down[i * STACK : (i + 1) * STACK, PW:] for i in range(3)]
    packed = jnp.concatenate([down[:, :PW], jnp.concatenate(tail, axis=1)], axis=0).astype(BF)
    for i in range(NZ):
        out_ref[i, SH:, :] = packed
        out_ref[i, :SH, :FF] = gate_ref[...]
        out_ref[i, :SH, FF:] = up_ref[...]


def unpack_down(full, wide):
    for p in range(NZ * NX):
        block = full[p // NX, p % NX, SH:, :].astype(F32)
        wide[p * FD : (p + 1) * FD, :PW] = block[:FD]
        for i in range(3):
            at = p * FD + i * STACK
            wide[at : at + STACK, PW:] = block[FD:, i * TW : (i + 1) * TW]


def pack_down(wide, grads):
    for p in range(NZ * NX):
        at = p * FD
        tail = [wide[at + i * STACK : at + (i + 1) * STACK, PW:] for i in range(3)]
        rows = jnp.concatenate([wide[at : at + FD, :PW], jnp.concatenate(tail, axis=1)], axis=0)
        grads[p // NX, p % NX, SH:, :] = rows.astype(BF)


def dispatch_kernel(ids_ref, weights_ref, tokens_ref, upstream_ref, keep_ref, give_ref):
    live, weight, mask = place(ids_ref[...], weights_ref[...])
    picker = mask.astype(F32).astype(BF)
    row_weight = jnp.sum(jnp.where(mask, weight, 0.0), axis=1, keepdims=True)
    rows = nn(picker, tokens_ref[...]).astype(BF)
    scaled = (row_weight * nn(picker, upstream_ref[...])).astype(BF)
    keep_ref[:, :D] = rows[: ROWS // 2]
    keep_ref[:, D:] = scaled[: ROWS // 2]
    give_ref[:, :D] = rows[ROWS // 2 :]
    give_ref[:, D:] = scaled[ROWS // 2 :]


def merge_kernel(keep_ref, got_ref, out_ref, sems):
    core = lax.axis_index("expert") % 2
    copies = [
        pltpu.make_async_copy(keep_ref, out_ref.at[:, core], sems.at[0]),
        pltpu.make_async_copy(got_ref, out_ref.at[:, 1 - core], sems.at[1]),
    ]
    for copy in copies:
        copy.start()
    for copy in copies:
        copy.wait()


def give_kernel(home_ref, after_ref, give_ref, sem):
    del after_ref
    core = lax.axis_index("expert") % 2
    copy = pltpu.make_async_copy(home_ref.at[:, 1 - core], give_ref, sem)
    copy.start()
    copy.wait()


def expert_kernel(*refs):
    recv_ref, near_ref, *far_refs = refs[:4]
    (sent_ref, q_own, q_right_lo, q_right_hi, q_left_lo, q_left_hi, q_far_lo, q_far_hi) = refs[4:12]
    sent, full, grads, wide, sems = refs[12:]
    x = lax.axis_index("dp") % NX
    to_right, to_left, across = (lax.rem(x + k, NX) for k in (1, NX - 1, 2))
    every = pl.ds(0, NZ)

    def spots(buffer, cut):
        low, high = pl.ds(0, cut), pl.ds(cut, NZ - cut)
        return (
            buffer.at[every, x],
            buffer.at[low, to_left],
            buffer.at[high, to_right],
            buffer.at[high, to_left],
            buffer.at[low, to_right],
            buffer.at[low, across],
            buffer.at[high, across],
        )

    pieces, start = [], 0
    for length in (NZ, LO, NZ - LO, NZ - LO, LO):
        pieces.append(near_ref.at[pl.ds(start, length)])
        start += length
    pieces += far_refs
    fetches = []
    for i, (piece, spot) in enumerate(zip(pieces, spots(full, LO))):
        fetches.append(pltpu.make_async_copy(piece, spot, sems.at[1 + i]))
    for fetch in fetches:
        fetch.start()
    for fetch in fetches:
        fetch.wait()

    gate = full[:, :, :SH, :FF].reshape(D, FF)
    up = full[:, :, :SH, FF:].reshape(D, FF)
    unpack_down(full, wide)
    down = wide[...].astype(BF)
    rows, scaled = recv_ref[:, :D], recv_ref[:, D:]
    pre_gate = nn(rows, gate)
    pre_up = nn(rows, up)
    grad_hidden = nt(scaled, down)
    sigma = jax.nn.sigmoid(pre_gate)
    silu = pre_gate * sigma
    hidden = (silu * pre_up).astype(BF)
    sent[:, :D] = nn(hidden, down).astype(BF)
    grad_gate_pre = (grad_hidden * pre_up * sigma * (1.0 + pre_gate * (1.0 - sigma))).astype(BF)
    grad_up_pre = (grad_hidden * silu).astype(BF)
    sent[:, D:] = (nt(grad_gate_pre, gate) + nt(grad_up_pre, up)).astype(BF)
    stores = [pltpu.make_async_copy(sent, sent_ref, sems.at[0])]
    stores[0].start()
    grads[:, :, :SH, :FF] = tn(rows, grad_gate_pre).astype(BF).reshape(NZ, NX, SH, FF)
    grads[:, :, :SH, FF:] = tn(rows, grad_up_pre).astype(BF).reshape(NZ, NX, SH, FF)
    wide[...] = tn(hidden, scaled)
    pack_down(wide, grads)
    pieces = (q_own, q_left_lo, q_right_hi, q_left_hi, q_right_lo, q_far_lo, q_far_hi)
    for i, (piece, spot) in enumerate(zip(pieces, spots(grads, NZ // 2))):
        stores.append(pltpu.make_async_copy(spot, piece, sems.at[1 + i]))
        stores[-1].start()
    for store in stores:
        store.wait()


def add_far_kernel(right_ref, left_ref, low_ref, high_ref, to_right_ref, to_left_ref):
    to_right_ref[...] = (right_ref[...].astype(F32) + low_ref[...].astype(F32)).astype(BF)
    to_left_ref[...] = (left_ref[...].astype(F32) + high_ref[...].astype(F32)).astype(BF)


def sum_x_kernel(own_ref, left_lo, left_hi, right_lo, right_hi, after_ref, out_ref):
    del after_ref
    h = NZ // 2
    low = left_lo[...].astype(F32) + right_lo[...].astype(F32)
    out_ref[:h] = (own_ref[:h].astype(F32) + low).astype(BF)
    high = left_hi[...].astype(F32) + right_hi[...].astype(F32)
    out_ref[h:] = (own_ref[h:].astype(F32) + high).astype(BF)


def sum_z_kernel(parts_ref, gate_ref, up_ref, down_ref):
    total = parts_ref[0].astype(F32)
    for z in range(1, NZ):
        total = total + parts_ref[z].astype(F32)
    gate_ref[...] = total[:SH, :FF].astype(BF)
    up_ref[...] = total[:SH, FF:].astype(BF)
    tail = [total[SH + FD :, i * TW : (i + 1) * TW] for i in range(3)]
    down_ref[:, :PW] = total[SH : SH + FD, :].astype(BF)
    down_ref[:, PW:] = jnp.concatenate(tail, axis=0).astype(BF)


def combine_kernel(
    ids_ref, weights_ref, upstream_ref, home_ref, got_ref, mixed_ref, tokens_ref, route_ref, rows, sems
):
    core = lax.axis_index("expert") % 2
    copies = [
        pltpu.make_async_copy(home_ref.at[:, core], rows.at[0], sems.at[0]),
        pltpu.make_async_copy(got_ref, rows.at[1], sems.at[1]),
    ]
    for copy in copies:
        copy.start()
    live, weight, mask = place(ids_ref[...], weights_ref[...])
    picker = mask.astype(F32).astype(BF)
    for copy in copies:
        copy.wait()
    home = rows[...].reshape(ROWS, 2 * D)
    tokens_ref[...] = tn(picker, home[:, D:]).astype(BF)
    picked = tn(picker, home[:, :D])
    mixed_ref[...] = (column_of(weight) * picked).astype(BF)
    inner = jnp.sum(upstream_ref[...].astype(F32) * picked, axis=1, keepdims=True)
    route_ref[...] = jnp.where(live, row_of(inner), 0.0)


def call(kernel, outs, scratch=(), vmem=16 * MIB, flops=0, moved=MIB, spaces=None, out_spaces=None):
    shapes = [jax.ShapeDtypeStruct(s, t) for s, t in outs]
    single = len(shapes) == 1
    specs = {}
    if spaces is not None:
        specs["in_specs"] = [pl.BlockSpec(memory_space=a or pltpu.VMEM) for a in spaces]
    if out_spaces is not None:
        specs["out_specs"] = [pl.BlockSpec(memory_space=a) for a in out_spaces]
        if single:
            specs["out_specs"] = specs["out_specs"][0]
    return pl.pallas_call(
        kernel,
        out_shape=shapes[0] if single else shapes,
        scratch_shapes=list(scratch),
        compiler_params=pltpu.CompilerParams(vmem_limit_bytes=vmem),
        cost_estimate=pl.CostEstimate(flops=flops, bytes_accessed=moved, transcendentals=0),
        **specs,
    )


Z_GROUPS = [[z * NX + x for z in range(NZ)] for x in range(NX)]


def swap_z(v):
    return lax.all_to_all(
        v, "dp", split_axis=0, concat_axis=0, tiled=True, axis_index_groups=Z_GROUPS
    )


def shift_x(v, k):
    pairs = [(z * NX + x, z * NX + (x + k) % NX) for z in range(NZ) for x in range(NX)]
    return lax.ppermute(v, "dp", pairs)


NY = FLIGHT // 2
Y_GROUPS = [[2 * y + core for y in range(NY)] for core in range(2)]


def swap_core(v):
    return lax.ppermute(v, "expert", [(i, i ^ 1) for i in range(FLIGHT)])


def exchange(v):
    return lax.all_to_all(
        v, "expert", split_axis=0, concat_axis=0, tiled=True, axis_index_groups=Y_GROUPS
    )


def on_device(tokens, route_ids, route_weights, upstream, w_gate, w_up, w_down):
    ids_t, weights_t = route_ids.T, route_weights.T
    copies = call(pack_kernel, [((NZ, PH, PW), BF)], vmem=58 * MIB)(w_gate[0], w_up[0], w_down[0])
    both, one = ((NY, 2, CAP, 2 * D), BF), ((NY, CAP, 2 * D), BF)
    keep, give = call(
        dispatch_kernel, [((ROWS // 2, 2 * D), BF)] * 2, vmem=58 * MIB, flops=4 * ROWS * TOK * D
    )(ids_t, weights_t, tokens, upstream)
    sent = call(
        merge_kernel,
        [both],
        scratch=[pltpu.SemaphoreType.DMA((2,))],
        spaces=(pl.ANY, pl.ANY),
        out_spaces=(pl.ANY,),
    )(keep.reshape(one[0]), swap_core(give).reshape(one[0]))
    own = swap_z(copies)
    recv = exchange(sent).reshape(ROWS, 2 * D)
    half = NZ // 2
    low, high = own[:LO], own[LO:]
    left_lo, right_hi = shift_x(low, 1), shift_x(high, NX - 1)
    left_hi, right_lo = shift_x(high, 1), shift_x(low, NX - 1)
    far_lo, far_hi = shift_x(left_lo, 1), shift_x(right_hi, NX - 1)
    whole, part = ((NZ, PH, PW), BF), ((half, PH, PW), BF)
    tile = pltpu.VMEM((ROWS, 2 * D), BF)
    matrix = pltpu.VMEM((NZ, NX, PH, PW), BF)
    back, q_own, q_right_lo, q_right_hi, q_left_lo, q_left_hi, q_far_lo, q_far_hi = call(
        expert_kernel,
        [((ROWS, 2 * D), BF), whole] + [part] * 6,
        scratch=[
            tile,
            matrix,
            matrix,
            pltpu.VMEM((FF, D), F32),
            pltpu.SemaphoreType.DMA((8,)),
        ],
        vmem=48 * MIB,
        flops=18 * ROWS * D * FF,
        moved=8 * MIB,
        spaces=(None,) + (pl.ANY,) * 3,
        out_spaces=(pl.ANY,) * 8,
    )(
        recv,
        jnp.concatenate([own, left_lo, right_hi, left_hi, right_lo], axis=0),
        far_lo,
        far_hi,
    )
    home = exchange(back.reshape(both[0]))
    add_lo, add_hi = shift_x(q_far_lo, 1), shift_x(q_far_hi, NX - 1)
    from_left_hi, from_right_lo = shift_x(q_right_hi, 1), shift_x(q_left_lo, NX - 1)
    to_right, to_left = call(add_far_kernel, [part, part], moved=2 * MIB)(
        q_right_lo, q_left_hi, add_lo, add_hi
    )
    from_left_lo, from_right_hi = shift_x(to_right, 1), shift_x(to_left, NX - 1)
    total = call(sum_x_kernel, [whole], moved=3 * MIB, spaces=(None,) * 5 + (pl.ANY,))(
        q_own, from_left_lo, from_left_hi, from_right_lo, from_right_hi, home
    )
    got = swap_core(
        call(
            give_kernel,
            [one],
            scratch=[pltpu.SemaphoreType.DMA],
            spaces=(pl.ANY, pl.ANY),
            out_spaces=(pl.ANY,),
        )(home, total)
    )
    parts = swap_z(total)
    grad_gate, grad_up, grad_down = call(
        sum_z_kernel, [((SH, FF), BF), ((SH, FF), BF), ((FD, D), BF)]
    )(parts)
    mixed, grad_tokens, grad_route = call(
        combine_kernel,
        [((TOK, D), BF), ((TOK, D), BF), ((8, TOK), F32)],
        scratch=[pltpu.VMEM((2,) + one[0], BF), pltpu.SemaphoreType.DMA((2,))],
        flops=4 * ROWS * TOK * D,
        moved=2 * MIB,
        spaces=(None, None, None, pl.ANY, pl.ANY),
    )(ids_t, weights_t, upstream, home, got)
    return (mixed, grad_tokens, grad_route.T, grad_gate[None], grad_up[None], grad_down[None])


def solution(mesh):
    rows, held = P(("dp", "expert"), None), P("expert", "dp", None)
    return jax.shard_map(
        on_device,
        mesh=mesh,
        in_specs=(rows, rows, rows, rows, held, held, held),
        out_specs=(rows, rows, rows, held, held, held),
        check_vma=False,
    )
```

```python
import jax
import jax.numpy as jnp
from jax import lax
from jax.experimental import pallas as pl
from jax.experimental.pallas import tpu as pltpu
from jax.sharding import PartitionSpec as P

FLIGHT = 16
CAP = 16
NZ = 8
NX = 4
TOK = 128
D = 1024
FF = 384
ROWS = FLIGHT * CAP
FD = FF // (NZ * NX)
SH = D // (NZ * NX)
PW = 2 * FF
PH = SH + 16
TW = D - PW
STACK = FD // 3
LO = 3
BF = jnp.bfloat16
F32 = jnp.float32
MIB = 1 << 20


def dot(a, b, dims):
    return lax.dot_general(a, b, (dims, ((), ())), preferred_element_type=F32)


def nn(a, b):
    return dot(a, b, ((1,), (0,)))


def tn(a, b):
    return dot(a, b, ((0,), (0,)))


def nt(a, b):
    return dot(a, b, ((1,), (1,)))


def route_rows(ids_t, weights_t):
    live = ids_t < FLIGHT
    expert = jnp.sum(jnp.where(live, ids_t, 0), axis=0, keepdims=True)
    weight = jnp.sum(jnp.where(live, weights_t, 0.0), axis=0, keepdims=True)
    alive = jnp.max(live.astype(jnp.int32), axis=0, keepdims=True) > 0
    return live, expert, weight, alive


def place(ids_t, weights_t):
    live, expert, weight, alive = route_rows(ids_t, weights_t)
    named = (lax.broadcasted_iota(jnp.int32, (FLIGHT, TOK), 0) == expert) & alive
    before = lax.broadcasted_iota(jnp.int32, (TOK, TOK), 0) < lax.broadcasted_iota(
        jnp.int32, (TOK, TOK), 1
    )
    rank = nn(named.astype(F32).astype(BF), before.astype(F32).astype(BF))
    slot = jnp.sum(jnp.where(named, rank, 0.0), axis=0, keepdims=True).astype(jnp.int32)
    core = lax.axis_index("expert") % 2
    row = jnp.where(expert % 2 == core, 0, ROWS // 2) + (expert // 2) * CAP + slot
    mask = lax.broadcasted_iota(jnp.int32, (ROWS, TOK), 0) == jnp.where(alive, row, -1)
    return live, weight, mask


def column_of(row):
    eye = lax.broadcasted_iota(jnp.int32, (TOK, TOK), 0) == lax.broadcasted_iota(
        jnp.int32, (TOK, TOK), 1
    )
    return jnp.sum(jnp.where(eye, row, 0.0), axis=1, keepdims=True)


def row_of(column):
    eye = lax.broadcasted_iota(jnp.int32, (TOK, TOK), 0) == lax.broadcasted_iota(
        jnp.int32, (TOK, TOK), 1
    )
    return jnp.sum(jnp.where(eye, column, 0.0), axis=0, keepdims=True)


def pack_kernel(gate_ref, up_ref, down_ref, out_ref):
    down = down_ref[...].astype(F32)
    tail = [down[i * STACK : (i + 1) * STACK, PW:] for i in range(3)]
    packed = jnp.concatenate([down[:, :PW], jnp.concatenate(tail, axis=1)], axis=0).astype(BF)
    for i in range(NZ):
        out_ref[i, SH:, :] = packed
        out_ref[i, :SH, :FF] = gate_ref[...]
        out_ref[i, :SH, FF:] = up_ref[...]


def unpack_down(full, wide):
    for p in range(NZ * NX):
        block = full[p // NX, p % NX, SH:, :].astype(F32)
        wide[p * FD : (p + 1) * FD, :PW] = block[:FD]
        for i in range(3):
            at = p * FD + i * STACK
            wide[at : at + STACK, PW:] = block[FD:, i * TW : (i + 1) * TW]


def pack_down(wide, grads):
    for p in range(NZ * NX):
        at = p * FD
        tail = [wide[at + i * STACK : at + (i + 1) * STACK, PW:] for i in range(3)]
        rows = jnp.concatenate([wide[at : at + FD, :PW], jnp.concatenate(tail, axis=1)], axis=0)
        grads[p // NX, p % NX, SH:, :] = rows.astype(BF)


def dispatch_kernel(ids_ref, weights_ref, tokens_ref, upstream_ref, keep_ref, give_ref):
    live, weight, mask = place(ids_ref[...], weights_ref[...])
    picker = mask.astype(F32).astype(BF)
    row_weight = jnp.sum(jnp.where(mask, weight, 0.0), axis=1, keepdims=True)
    rows = nn(picker, tokens_ref[...]).astype(BF)
    scaled = (row_weight * nn(picker, upstream_ref[...])).astype(BF)
    keep_ref[:, :D] = rows[: ROWS // 2]
    keep_ref[:, D:] = scaled[: ROWS // 2]
    give_ref[:, :D] = rows[ROWS // 2 :]
    give_ref[:, D:] = scaled[ROWS // 2 :]


def merge_kernel(keep_ref, got_ref, out_ref, sems):
    core = lax.axis_index("expert") % 2
    copies = [
        pltpu.make_async_copy(keep_ref, out_ref.at[:, core], sems.at[0]),
        pltpu.make_async_copy(got_ref, out_ref.at[:, 1 - core], sems.at[1]),
    ]
    for copy in copies:
        copy.start()
    for copy in copies:
        copy.wait()


def give_kernel(home_ref, after_ref, give_ref, sem):
    del after_ref
    core = lax.axis_index("expert") % 2
    copy = pltpu.make_async_copy(home_ref.at[:, 1 - core], give_ref, sem)
    copy.start()
    copy.wait()


def expert_kernel(*refs):
    recv_ref, near_ref, *far_refs = refs[:4]
    (sent_ref, q_own, q_right_lo, q_right_hi, q_left_lo, q_left_hi, q_far_lo, q_far_hi) = refs[4:12]
    sent, full, grads, wide, sems = refs[12:]
    x = lax.axis_index("dp") % NX
    to_right, to_left, across = (lax.rem(x + k, NX) for k in (1, NX - 1, 2))
    every = pl.ds(0, NZ)

    def spots(buffer, cut):
        low, high = pl.ds(0, cut), pl.ds(cut, NZ - cut)
        return (
            buffer.at[every, x],
            buffer.at[low, to_left],
            buffer.at[high, to_right],
            buffer.at[high, to_left],
            buffer.at[low, to_right],
            buffer.at[low, across],
            buffer.at[high, across],
        )

    pieces, start = [], 0
    for length in (NZ, LO, NZ - LO, NZ - LO, LO):
        pieces.append(near_ref.at[pl.ds(start, length)])
        start += length
    pieces += far_refs
    fetches = []
    for i, (piece, spot) in enumerate(zip(pieces, spots(full, LO))):
        fetches.append(pltpu.make_async_copy(piece, spot, sems.at[1 + i]))
    for fetch in fetches:
        fetch.start()
    for fetch in fetches:
        fetch.wait()

    gate = full[:, :, :SH, :FF].reshape(D, FF)
    up = full[:, :, :SH, FF:].reshape(D, FF)
    unpack_down(full, wide)
    down = wide[...].astype(BF)
    rows, scaled = recv_ref[:, :D], recv_ref[:, D:]
    pre_gate = nn(rows, gate)
    pre_up = nn(rows, up)
    grad_hidden = nt(scaled, down)
    sigma = jax.nn.sigmoid(pre_gate)
    silu = pre_gate * sigma
    hidden = (silu * pre_up).astype(BF)
    sent[:, :D] = nn(hidden, down).astype(BF)
    grad_gate_pre = (grad_hidden * pre_up * sigma * (1.0 + pre_gate * (1.0 - sigma))).astype(BF)
    grad_up_pre = (grad_hidden * silu).astype(BF)
    sent[:, D:] = (nt(grad_gate_pre, gate) + nt(grad_up_pre, up)).astype(BF)
    stores = [pltpu.make_async_copy(sent, sent_ref, sems.at[0])]
    stores[0].start()
    grads[:, :, :SH, :FF] = tn(rows, grad_gate_pre).astype(BF).reshape(NZ, NX, SH, FF)
    grads[:, :, :SH, FF:] = tn(rows, grad_up_pre).astype(BF).reshape(NZ, NX, SH, FF)
    wide[...] = tn(hidden, scaled)
    pack_down(wide, grads)
    pieces = (q_own, q_left_lo, q_right_hi, q_left_hi, q_right_lo, q_far_lo, q_far_hi)
    for i, (piece, spot) in enumerate(zip(pieces, spots(grads, NZ // 2))):
        stores.append(pltpu.make_async_copy(spot, piece, sems.at[1 + i]))
        stores[-1].start()
    for store in stores:
        store.wait()


def add_far_kernel(right_ref, left_ref, low_ref, high_ref, to_right_ref, to_left_ref):
    to_right_ref[...] = (right_ref[...].astype(F32) + low_ref[...].astype(F32)).astype(BF)
    to_left_ref[...] = (left_ref[...].astype(F32) + high_ref[...].astype(F32)).astype(BF)


def sum_x_kernel(own_ref, left_lo, left_hi, right_lo, right_hi, after_ref, out_ref, total, sems):
    del after_ref
    half, copies = NZ // 2, []
    for z in range(NZ):
        left, right = (left_lo, right_lo) if z < half else (left_hi, right_hi)
        met = left[z % half].astype(F32) + right[z % half].astype(F32)
        total[z] = (own_ref[z].astype(F32) + met).astype(BF)
        copies.append(pltpu.make_async_copy(total.at[z], out_ref.at[z], sems.at[z]))
        copies[-1].start()
    for copy in copies:
        copy.wait()


def sum_z_kernel(parts_ref, gate_ref, up_ref, down_ref):
    total = parts_ref[0].astype(F32)
    for z in range(1, NZ):
        total = total + parts_ref[z].astype(F32)
    gate_ref[...] = total[:SH, :FF].astype(BF)
    up_ref[...] = total[:SH, FF:].astype(BF)
    tail = [total[SH + FD :, i * TW : (i + 1) * TW] for i in range(3)]
    down_ref[:, :PW] = total[SH : SH + FD, :].astype(BF)
    down_ref[:, PW:] = jnp.concatenate(tail, axis=0).astype(BF)


def combine_kernel(
    ids_ref, weights_ref, upstream_ref, home_ref, got_ref, mixed_ref, tokens_ref, route_ref, rows, sems
):
    core = lax.axis_index("expert") % 2
    copies = [
        pltpu.make_async_copy(home_ref.at[:, core], rows.at[0], sems.at[0]),
        pltpu.make_async_copy(got_ref, rows.at[1], sems.at[1]),
    ]
    for copy in copies:
        copy.start()
    live, weight, mask = place(ids_ref[...], weights_ref[...])
    picker = mask.astype(F32).astype(BF)
    for copy in copies:
        copy.wait()
    home = rows[...].reshape(ROWS, 2 * D)
    tokens_ref[...] = tn(picker, home[:, D:]).astype(BF)
    picked = tn(picker, home[:, :D])
    mixed_ref[...] = (column_of(weight) * picked).astype(BF)
    inner = jnp.sum(upstream_ref[...].astype(F32) * picked, axis=1, keepdims=True)
    route_ref[...] = jnp.where(live, row_of(inner), 0.0)


def call(kernel, outs, scratch=(), vmem=16 * MIB, flops=0, moved=MIB, spaces=None, out_spaces=None):
    shapes = [jax.ShapeDtypeStruct(s, t) for s, t in outs]
    single = len(shapes) == 1
    specs = {}
    if spaces is not None:
        specs["in_specs"] = [pl.BlockSpec(memory_space=a or pltpu.VMEM) for a in spaces]
    if out_spaces is not None:
        specs["out_specs"] = [pl.BlockSpec(memory_space=a) for a in out_spaces]
        if single:
            specs["out_specs"] = specs["out_specs"][0]
    return pl.pallas_call(
        kernel,
        out_shape=shapes[0] if single else shapes,
        scratch_shapes=list(scratch),
        compiler_params=pltpu.CompilerParams(vmem_limit_bytes=vmem),
        cost_estimate=pl.CostEstimate(flops=flops, bytes_accessed=moved, transcendentals=0),
        **specs,
    )


Z_GROUPS = [[z * NX + x for z in range(NZ)] for x in range(NX)]


def swap_z(v):
    return lax.all_to_all(
        v, "dp", split_axis=0, concat_axis=0, tiled=True, axis_index_groups=Z_GROUPS
    )


def shift_x(v, k):
    pairs = [(z * NX + x, z * NX + (x + k) % NX) for z in range(NZ) for x in range(NX)]
    return lax.ppermute(v, "dp", pairs)


NY = FLIGHT // 2
Y_GROUPS = [[2 * y + core for y in range(NY)] for core in range(2)]


def swap_core(v):
    return lax.ppermute(v, "expert", [(i, i ^ 1) for i in range(FLIGHT)])


def exchange(v):
    return lax.all_to_all(
        v, "expert", split_axis=0, concat_axis=0, tiled=True, axis_index_groups=Y_GROUPS
    )


def on_device(tokens, route_ids, route_weights, upstream, w_gate, w_up, w_down):
    ids_t, weights_t = route_ids.T, route_weights.T
    copies = call(pack_kernel, [((NZ, PH, PW), BF)], vmem=58 * MIB)(w_gate[0], w_up[0], w_down[0])
    both, one = ((NY, 2, CAP, 2 * D), BF), ((NY, CAP, 2 * D), BF)
    keep, give = call(
        dispatch_kernel, [((ROWS // 2, 2 * D), BF)] * 2, vmem=58 * MIB, flops=4 * ROWS * TOK * D
    )(ids_t, weights_t, tokens, upstream)
    sent = call(
        merge_kernel,
        [both],
        scratch=[pltpu.SemaphoreType.DMA((2,))],
        spaces=(pl.ANY, pl.ANY),
        out_spaces=(pl.ANY,),
    )(keep.reshape(one[0]), swap_core(give).reshape(one[0]))
    own = swap_z(copies)
    recv = exchange(sent).reshape(ROWS, 2 * D)
    half = NZ // 2
    low, high = own[:LO], own[LO:]
    left_lo, right_hi = shift_x(low, 1), shift_x(high, NX - 1)
    left_hi, right_lo = shift_x(high, 1), shift_x(low, NX - 1)
    far_lo, far_hi = shift_x(left_lo, 1), shift_x(right_hi, NX - 1)
    whole, part = ((NZ, PH, PW), BF), ((half, PH, PW), BF)
    tile = pltpu.VMEM((ROWS, 2 * D), BF)
    matrix = pltpu.VMEM((NZ, NX, PH, PW), BF)
    back, q_own, q_right_lo, q_right_hi, q_left_lo, q_left_hi, q_far_lo, q_far_hi = call(
        expert_kernel,
        [((ROWS, 2 * D), BF), whole] + [part] * 6,
        scratch=[
            tile,
            matrix,
            matrix,
            pltpu.VMEM((FF, D), F32),
            pltpu.SemaphoreType.DMA((8,)),
        ],
        vmem=48 * MIB,
        flops=18 * ROWS * D * FF,
        moved=8 * MIB,
        spaces=(None,) + (pl.ANY,) * 3,
        out_spaces=(pl.ANY,) * 8,
    )(
        recv,
        jnp.concatenate([own, left_lo, right_hi, left_hi, right_lo], axis=0),
        far_lo,
        far_hi,
    )
    home = exchange(back.reshape(both[0]))
    add_lo, add_hi = shift_x(q_far_lo, 1), shift_x(q_far_hi, NX - 1)
    from_left_hi, from_right_lo = shift_x(q_right_hi, 1), shift_x(q_left_lo, NX - 1)
    to_right, to_left = call(add_far_kernel, [part, part], moved=2 * MIB)(
        q_right_lo, q_left_hi, add_lo, add_hi
    )
    from_left_lo, from_right_hi = shift_x(to_right, 1), shift_x(to_left, NX - 1)
    total = call(
        sum_x_kernel,
        [whole],
        scratch=[pltpu.VMEM(whole[0], BF), pltpu.SemaphoreType.DMA((NZ,))],
        moved=3 * MIB,
        spaces=(None,) * 5 + (pl.ANY,),
        out_spaces=(pl.ANY,),
    )(
        q_own, from_left_lo, from_left_hi, from_right_lo, from_right_hi, home
    )
    got = swap_core(
        call(
            give_kernel,
            [one],
            scratch=[pltpu.SemaphoreType.DMA],
            spaces=(pl.ANY, pl.ANY),
            out_spaces=(pl.ANY,),
        )(home, total)
    )
    parts = swap_z(total)
    grad_gate, grad_up, grad_down = call(
        sum_z_kernel, [((SH, FF), BF), ((SH, FF), BF), ((FD, D), BF)]
    )(parts)
    mixed, grad_tokens, grad_route = call(
        combine_kernel,
        [((TOK, D), BF), ((TOK, D), BF), ((8, TOK), F32)],
        scratch=[pltpu.VMEM((2,) + one[0], BF), pltpu.SemaphoreType.DMA((2,))],
        flops=4 * ROWS * TOK * D,
        moved=2 * MIB,
        spaces=(None, None, None, pl.ANY, pl.ANY),
    )(ids_t, weights_t, upstream, home, got)
    return (mixed, grad_tokens, grad_route.T, grad_gate[None], grad_up[None], grad_down[None])


def solution(mesh):
    rows, held = P(("dp", "expert"), None), P("expert", "dp", None)
    return jax.shard_map(
        on_device,
        mesh=mesh,
        in_specs=(rows, rows, rows, rows, held, held, held),
        out_specs=(rows, rows, rows, held, held, held),
        check_vma=False,
    )
```
